1024 devices in a mesh: dp: 256 (over x, z, y_hi), pipe: 4 (over y_lo, core).
Axes of the slice: x: 4, y: 4 (y_hi: 2, y_lo: 2; y = y_hi * 2 + y_lo), z: 32, core: 2. Of those that a mesh axis runs over, the one named last changes fastest.
Arguments:
- text_states: bfloat16 [4, 16384, 4096], P('pipe', 'dp')
- image_states: bfloat16 [4, 16384, 4096], P(None, ('dp', 'pipe'))
- image_start: int32 [4, 256], P(None, 'dp'), may hold values from 0 to 31
- w_query: bfloat16 [4, 4096, 512], P('pipe')
- w_key: bfloat16 [4, 4096, 128], P('pipe', 'dp')
- w_value: bfloat16 [4, 4096, 128], P('pipe', 'dp'), may hold values from -0.09375 to 0.09375
- w_out: bfloat16 [4, 512, 4096], P('pipe'), may hold values from -0.25 to 0.25
- query_gain: float32 [4, 128], P('pipe'), may hold values from 1 to 2.5
- key_gain: float32 [4, 128], P('pipe'), may hold values from 1 to 2
- cross_gate: float32 [4], P('pipe'), may hold values from 0.3 to 1.2
Outputs:
- final_states: bfloat16 [4, 16384, 4096], P('pipe', 'dp')
The draws below stay inside these ranges and needn't reach their ends.
All inputs are finite; a program needn't handle non-finite values.
Results may differ from the reference program's by a relative error of at most 0.013.
Values may be sent and summed in bfloat16 or wider, within the bound.
No kernel may reach another device: no remote copies, remote signals or barrier semaphores. Data moves between devices by JAX's collectives and lax.ppermute only.
A program may use at most 64 MiB of HBM per device.

```python
import math
import jax
import jax.numpy as jnp
from jax import lax

D = 4096
HD = 128
QH = 4
TOK_DEV = 64
MICRO = 4
TOKENS = 16384
IMG_GROUP = 64
IMAGES = 16384
N_DP = 256
N_PIPE = 4


def draw_text_states(key, part):
    key = jax.random.fold_in(key, 11)
    first, second, third = jax.random.split(key, 3)
    shape = (MICRO, TOKENS, D)
    base = jnp.clip(jax.random.normal(first, shape, jnp.float32), -4.0, 4.0)
    rows = jnp.exp(jax.random.uniform(second, (MICRO, TOKENS, 1), jnp.float32, math.log(0.5), math.log(4.0)))
    columns = jnp.exp(jax.random.uniform(third, (1, 1, D), jnp.float32, math.log(0.5), math.log(2.0)))
    return (base * rows * columns).astype(jnp.bfloat16)


def draw_image_states(key, part):
    key = jax.random.fold_in(key, 12)
    first, second, third = jax.random.split(key, 3)
    shape = (MICRO, IMAGES, D)
    base = jnp.clip(jax.random.normal(first, shape, jnp.float32), -4.0, 4.0)
    rows = jnp.exp(jax.random.uniform(second, (MICRO, IMAGES, 1), jnp.float32, math.log(0.5), math.log(4.0)))
    columns = jnp.exp(jax.random.uniform(third, (1, 1, D), jnp.float32, math.log(0.5), math.log(2.0)))
    return (base * rows * columns).astype(jnp.bfloat16)


def draw_w_query(key, part):
    key = jax.random.fold_in(key, 13)
    first, second = jax.random.split(key, 2)
    shape = (N_PIPE, D, QH * HD)
    base = jnp.clip(jax.random.normal(first, shape, jnp.float32), -4.0, 4.0)
    columns = jnp.exp(jax.random.uniform(second, (N_PIPE, 1, QH * HD), jnp.float32, 0.0, math.log(10.0)))
    return (base * columns / math.sqrt(D)).astype(jnp.bfloat16)


def draw_w_key(key, part):
    key = jax.random.fold_in(key, 14)
    first, second = jax.random.split(key, 2)
    shape = (N_PIPE, D, HD)
    base = jnp.clip(jax.random.normal(first, shape, jnp.float32), -4.0, 4.0)
    columns = jnp.exp(jax.random.uniform(second, (N_PIPE, 1, HD), jnp.float32, 0.0, math.log(10.0)))
    return (base * columns / math.sqrt(D)).astype(jnp.bfloat16)


def touch_ends(values, rng, least, top_value):
    dims = values.shape
    place = [jax.random.randint(jax.random.fold_in(rng, axis), (), 0, dims[axis]) for axis in range(len(dims))]
    values = values.at[tuple(place)].set(least)
    longest = dims.index(max(dims))
    place[longest] = (place[longest] + 1) % dims[longest]
    return values.at[tuple(place)].set(top_value)


def level_of(key, shape, shards, low, high):
    def one(position, blocks):
        draws = jax.random.uniform(jax.random.fold_in(jax.random.fold_in(key, 6), position), (blocks,), jnp.float32, low / len(shards), high / len(shards))
        return jnp.repeat(jnp.exp(draws), shape[position] // blocks).reshape((-1,) + (1,) * (len(shape) - position - 1))

    gain = one(*shards[0])
    for cut in shards[1:]:
        gain = gain * one(*cut)
    return gain


def centred(rng, dims, width, most, cuts=(), kind=jnp.bfloat16):
    result = jax.random.normal(rng, dims, jnp.float32) * width
    if len(cuts) > 0:
        result = level_of(rng, dims, cuts, -0.22, 0.18) * result
    return jnp.clip(result, min=-most, max=most).astype(kind)


def setup_inputs(seed: int = 0) -> dict:
    seeds = jax.random.split(jax.random.key(seed), 11)
    text_states = draw_text_states(jax.random.fold_in(seeds[10], 71), 0)
    image_states = draw_image_states(jax.random.fold_in(seeds[10], 71), 0)
    image_start = touch_ends(jax.random.randint(seeds[2], (MICRO, N_DP), 0, TOK_DEV // 2), jax.random.fold_in(seeds[2], 1), 0, (TOK_DEV // 2) - 1).astype(jnp.int32)
    w_query = draw_w_query(jax.random.fold_in(seeds[10], 71), 0)
    w_key = draw_w_key(jax.random.fold_in(seeds[10], 71), 0)
    w_value = centred(seeds[5], (N_PIPE, D, HD), D ** -0.5, 0.09375, ((0, 4), (1, 256)))
    w_out = centred(seeds[6], (N_PIPE, QH * HD, D), (QH * HD) ** -0.5, 0.25, ((0, 4),))
    query_gain = jnp.clip(1.0 + 1.5 * jax.random.uniform(seeds[7], (N_PIPE, HD), jnp.float32) ** level_of(seeds[7], (N_PIPE, HD), ((0, 4),), -0.2, 0.2), 1.0, 2.5)
    key_gain = jnp.clip(1.0 + 1.0 * jax.random.uniform(seeds[8], (N_PIPE, HD), jnp.float32) ** level_of(seeds[8], (N_PIPE, HD), ((0, 4),), -0.2, 0.2), 1.0, 2.0)
    cross_gate = jnp.clip(0.3 + 0.90000004 * jax.random.uniform(seeds[9], (N_PIPE,), jnp.float32) ** level_of(seeds[9], (N_PIPE,), ((0, 4),), -0.2, 0.2), 0.3, 1.2)
    return dict(text_states=text_states, image_states=image_states, image_start=image_start, w_query=w_query, w_key=w_key, w_value=w_value, w_out=w_out, query_gain=query_gain, key_gain=key_gain, cross_gate=cross_gate)


epsilon = 1e-06

def normalized(projected, scales):
    mean_square = lax.optimization_barrier(jnp.mean(projected * projected, axis=-1, keepdims=True))
    return projected * lax.rsqrt(mean_square + epsilon) * scales

def reference(text_states, image_states, image_start, w_query, w_key, w_value, w_out, query_gain, key_gain, cross_gate):
    positions = jnp.arange(TOK_DEV, dtype=jnp.int32)
    results = []
    for batch_index in range(MICRO):
        current = text_states[batch_index]
        pictures = image_states[batch_index]
        starts = image_start[batch_index].astype(jnp.int32)
        seen = (positions[None, :] >= starts[:, None]).astype(jnp.float32).reshape(TOKENS, 1)
        for layer_index in range(batch_index, N_PIPE):
            key_sums = jnp.dot(pictures, w_key[layer_index], preferred_element_type=jnp.float32)
            key_rows = normalized(key_sums, key_gain[layer_index]).astype(jnp.bfloat16).reshape(N_DP, IMG_GROUP, HD)
            value_rows = jnp.dot(pictures, w_value[layer_index], preferred_element_type=jnp.float32)
            value_rows = value_rows.astype(jnp.bfloat16).reshape(N_DP, IMG_GROUP, HD)
            query_sums = jnp.dot(current, w_query[layer_index], preferred_element_type=jnp.float32)
            query_sums = query_sums.reshape(N_DP, TOK_DEV, QH, HD)
            queries = normalized(query_sums, query_gain[layer_index]).astype(jnp.bfloat16)
            scores = jnp.einsum('gthc,gic->gthi', queries.astype(jnp.float32), key_rows.astype(jnp.float32)) / math.sqrt(HD)
            exponent = jnp.exp(scores)
            probs = (exponent / lax.optimization_barrier(jnp.sum(exponent, axis=-1, keepdims=True))).astype(jnp.bfloat16)
            attended = jnp.einsum('gthi,gic->gthc', probs.astype(jnp.float32), value_rows.astype(jnp.float32))
            attended = attended.astype(jnp.bfloat16).reshape(TOKENS, QH * HD)
            update = jnp.dot(attended, w_out[layer_index], preferred_element_type=jnp.float32)
            current = (current.astype(jnp.float32) + jnp.tanh(cross_gate[layer_index]) * seen * update).astype(jnp.bfloat16)
        results.append(current)
    return jnp.stack(results)
```

```python
import math

import jax
import jax.numpy as jnp
from jax import lax
from jax.sharding import Mesh
from jax.sharding import PartitionSpec as P

epsilon = 1e-06


def shifted(block, axis, distance):
    devices = range(lax.axis_size(axis))
    route = [((i - distance) % len(devices), i) for i in devices]
    return lax.ppermute(block, axis, route)


def normalized(projected, scales):
    mean_square = jnp.mean(projected * projected, axis=-1, keepdims=True)
    return projected * lax.rsqrt(mean_square + epsilon) * scales


def keep_state(current, holding):
    return current


def exchanged(block, axis, distance):
    devices = range(lax.axis_size(axis))
    return lax.ppermute(block, axis, [(i, i ^ distance) for i in devices])


def doubled(known, axis, distance, where):
    other = exchanged(known, axis, distance)
    upper = (lax.axis_index(axis) & distance) != 0
    first = jnp.where(upper, other, known)
    second = jnp.where(upper, known, other)
    return jnp.stack([first, second], axis=where)


def gathered_rows(shard):
    rows, columns = shard.shape
    known = doubled(shard[None], "yh", 1, 1)
    distance = lax.axis_size("z") // 2
    while distance >= 1:
        known = doubled(known, "z", distance, 1)
        known = known.reshape((-1,) + known.shape[2:])
        distance //= 2
    return known.reshape(-1, columns)


def column_slices(image_states):
    batches, rows, width = image_states.shape
    parts = lax.axis_size("x")
    own = lax.axis_index("x")
    cut = jnp.moveaxis(image_states.reshape(batches, rows, parts, width // parts), 2, 0)
    blocks = [
        exchanged(lax.dynamic_index_in_dim(cut, own ^ distance, 0, keepdims=False), "x", distance)
        if distance
        else lax.dynamic_index_in_dim(cut, own, 0, keepdims=False)
        for distance in range(parts)
    ]
    ordered = jnp.stack(blocks)
    ordered = jnp.take(ordered, own ^ jnp.arange(parts), axis=0)
    halves = doubled(ordered, "pipe", 2, 0)
    return doubled(halves, "pipe", 1, 1).reshape((-1,) + ordered.shape)


def local(
    text_states,
    image_states,
    image_start,
    w_query,
    w_key,
    w_value,
    w_out,
    query_gain,
    key_gain,
    cross_gate,
):
    sections = lax.axis_size("pipe")
    section_index = lax.axis_index("pipe")
    head_size = w_key.shape[2]
    head_count = w_query.shape[2] // head_size
    weights = gathered_rows(jnp.concatenate([w_key[0], w_value[0]], axis=1))
    pictures = column_slices(image_states)
    parts, depth = lax.axis_size("x"), weights.shape[0]
    sums = jnp.dot(pictures.reshape(-1, depth), weights, preferred_element_type=jnp.float32)
    sums = sums.reshape(pictures.shape[:-1] + (2 * head_size,))
    own = lax.axis_index("x")
    total = lax.dynamic_index_in_dim(sums, own, 1, keepdims=False)
    rounded = sums.astype(jnp.bfloat16)
    for distance in range(1, parts):
        block = lax.dynamic_index_in_dim(rounded, own ^ distance, 1, keepdims=False)
        total = total + exchanged(block, "x", distance).astype(jnp.float32)
    total = jnp.swapaxes(total, 0, 1)
    total = total.reshape(total.shape[0], -1, 2 * head_size)
    key_rows = normalized(total[..., :head_size], key_gain[0]).astype(jnp.bfloat16)
    value_rows = total[..., head_size:].astype(jnp.bfloat16)
    query_weight = w_query[0]
    out_weight = w_out[0]
    factor = jnp.tanh(cross_gate[0])
    tok_rows = text_states.shape[1]
    positions = jnp.arange(tok_rows, dtype=jnp.int32)
    root_size = math.sqrt(head_size)

    def apply_layer(current, holding):
        own_keys = lax.dynamic_index_in_dim(key_rows, holding, 0, keepdims=False)
        own_values = lax.dynamic_index_in_dim(value_rows, holding, 0, keepdims=False)
        query_sums = jnp.dot(current, query_weight, preferred_element_type=jnp.float32)
        query_sums = query_sums.reshape(tok_rows * head_count, head_size)
        queries = normalized(query_sums, query_gain[0]).astype(jnp.bfloat16)
        scores = jnp.dot(queries, own_keys.T, preferred_element_type=jnp.float32) / root_size
        exponent = jnp.exp(scores)
        probs = (exponent / jnp.sum(exponent, axis=-1, keepdims=True)).astype(jnp.bfloat16)
        attended = jnp.dot(probs, own_values, preferred_element_type=jnp.float32).astype(
            jnp.bfloat16
        )
        attended = attended.reshape(tok_rows, head_count * head_size)
        update = jnp.dot(attended, out_weight, preferred_element_type=jnp.float32)
        first_seen = lax.dynamic_index_in_dim(image_start[:, 0], holding, 0, keepdims=False)
        seen = (positions >= first_seen).astype(jnp.float32)[:, None]
        return (current.astype(jnp.float32) + factor * seen * update).astype(jnp.bfloat16)

    current = text_states[0]
    for moment in range(sections):
        holding = jnp.mod(section_index - moment, sections)
        current = lax.cond(moment <= section_index, apply_layer, keep_state, current, holding)
        current = shifted(current, "pipe", 1)
    return current[None]


def solution(mesh):
    sections = mesh.shape["pipe"]
    planes, far = 4, 2
    groups = mesh.shape["dp"] // (planes * far)
    mesh = Mesh(mesh.devices.reshape(planes, groups, far, sections), ("x", "z", "yh", "pipe"))
    replicas = ("x", "z", "yh")
    placed = (
        P("pipe", replicas, None),
        P(None, replicas + ("pipe",), None),
        P(None, replicas),
        P("pipe", None, None),
        P("pipe", replicas, None),
        P("pipe", replicas, None),
        P("pipe", None, None),
        P("pipe", None),
        P("pipe", None),
        P("pipe"),
    )
    return jax.shard_map(
        local, mesh=mesh, in_specs=placed, out_specs=P("pipe", replicas, None), check_vma=False
    )
```

```python
import functools
import math

import jax
import jax.numpy as jnp
from jax import lax
from jax.experimental import pallas as pl
from jax.experimental.pallas import tpu as pltpu
from jax.sharding import Mesh
from jax.sharding import PartitionSpec as P

epsilon = 1e-06


def shifted(block, axis, distance):
    devices = range(lax.axis_size(axis))
    route = [((i - distance) % len(devices), i) for i in devices]
    return lax.ppermute(block, axis, route)


def normalized(projected, scales):
    mean_square = jnp.mean(projected * projected, axis=-1, keepdims=True)
    return projected * lax.rsqrt(mean_square + epsilon) * scales


def layer_kernel(
    parts,
    moment_ref,
    first_seen_ref,
    factor_ref,
    current_ref,
    key_ref,
    value_ref,
    gain_ref,
    w_query_ref,
    w_out_ref,
    out_ref,
    query_weight,
    out_weight,
    sems,
):
    rows, width = current_ref.shape
    columns = w_query_ref.shape[1]
    head_size = key_ref.shape[2]
    heads = columns // head_size
    step = width // parts
    holding = moment_ref[0]
    active = moment_ref[1] == 1

    @pl.when(active)
    def _():
        copies = []
        for part in range(parts):
            piece = pl.ds(part * step, step)
            copies.append(
                pltpu.make_async_copy(
                    w_query_ref.at[piece, :], query_weight.at[piece, :], sems.at[0, part]
                )
            )
        for part in range(parts):
            piece = pl.ds(part * step, step)
            copies.append(
                pltpu.make_async_copy(
                    w_out_ref.at[:, piece], out_weight.at[:, piece], sems.at[1, part]
                )
            )
        for copy in copies:
            copy.start()
        query_sums = jnp.zeros((rows, columns), jnp.float32)
        for part in range(parts):
            copies[part].wait()
            piece = pl.ds(part * step, step)
            query_sums += jnp.dot(
                current_ref[:, piece], query_weight[piece, :], preferred_element_type=jnp.float32
            )
        stacked = jnp.concatenate(
            [query_sums[:, h * head_size : (h + 1) * head_size] for h in range(heads)], axis=0
        )
        queries = normalized(stacked, gain_ref[...]).astype(jnp.bfloat16)
        scores = lax.dot_general(
            queries,
            key_ref[holding],
            (((1,), (1,)), ((), ())),
            preferred_element_type=jnp.float32,
        ) / math.sqrt(head_size)
        exponent = jnp.exp(scores)
        probs = (exponent / jnp.sum(exponent, axis=-1, keepdims=True)).astype(jnp.bfloat16)
        attended = jnp.dot(probs, value_ref[holding], preferred_element_type=jnp.float32)
        attended = attended.astype(jnp.bfloat16)
        attended = jnp.concatenate(
            [attended[h * rows : (h + 1) * rows] for h in range(heads)], axis=1
        )
        positions = lax.broadcasted_iota(jnp.int32, (rows, 1), 0)
        scale = jnp.where(positions >= first_seen_ref[holding], factor_ref[0], 0.0)
        for part in range(parts):
            copies[parts + part].wait()
            piece = pl.ds(part * step, step)
            update = jnp.dot(attended, out_weight[:, piece], preferred_element_type=jnp.float32)
            state = current_ref[:, piece].astype(jnp.float32) + scale * update
            out_ref[:, piece] = state.astype(jnp.bfloat16)

    @pl.when(jnp.logical_not(active))
    def _():
        out_ref[...] = current_ref[...]


def layer(moment, first_seen, factor, current, key_rows, value_rows, gain, w_query, w_out):
    parts = 4
    rows, width = current.shape
    columns = w_query.shape[1]
    smem = pl.BlockSpec(memory_space=pltpu.SMEM)
    vmem = pl.BlockSpec(memory_space=pltpu.VMEM)
    return pl.pallas_call(
        functools.partial(layer_kernel, parts),
        out_shape=jax.ShapeDtypeStruct(current.shape, current.dtype),
        in_specs=[smem] * 3 + [vmem] * 4 + [pl.BlockSpec(memory_space=pl.ANY)] * 2,
        out_specs=vmem,
        scratch_shapes=[
            pltpu.VMEM(w_query.shape, w_query.dtype),
            pltpu.VMEM(w_out.shape, w_out.dtype),
            pltpu.SemaphoreType.DMA((2, parts)),
        ],
        compiler_params=pltpu.CompilerParams(vmem_limit_bytes=24 * 2**20),
        cost_estimate=pl.CostEstimate(
            flops=4 * rows * width * columns,
            bytes_accessed=4 * width * columns,
            transcendentals=rows * columns,
        ),
    )(moment, first_seen, factor, current, key_rows, value_rows, gain, w_query, w_out)


def exchanged(block, axis, distance):
    devices = range(lax.axis_size(axis))
    return lax.ppermute(block, axis, [(i, i ^ distance) for i in devices])


def doubled(known, axis, distance, where):
    other = exchanged(known, axis, distance)
    upper = (lax.axis_index(axis) & distance) != 0
    first = jnp.where(upper, other, known)
    second = jnp.where(upper, known, other)
    return jnp.stack([first, second], axis=where)


def gathered_rows(shard):
    rows, columns = shard.shape
    known = doubled(shard[None], "yh", 1, 1)
    distance = lax.axis_size("z") // 2
    while distance >= 1:
        known = doubled(known, "z", distance, 1)
        known = known.reshape((-1,) + known.shape[2:])
        distance //= 2
    return known.reshape(-1, columns)


def column_slices(image_states):
    batches, rows, width = image_states.shape
    parts = lax.axis_size("x")
    own = lax.axis_index("x")
    cut = jnp.moveaxis(image_states.reshape(batches, rows, parts, width // parts), 2, 0)
    blocks = [
        exchanged(lax.dynamic_index_in_dim(cut, own ^ distance, 0, keepdims=False), "x", distance)
        if distance
        else lax.dynamic_index_in_dim(cut, own, 0, keepdims=False)
        for distance in range(parts)
    ]
    ordered = jnp.stack(blocks)
    ordered = jnp.take(ordered, own ^ jnp.arange(parts), axis=0)
    halves = doubled(ordered, "pipe", 2, 0)
    return doubled(halves, "pipe", 1, 1).reshape((-1,) + ordered.shape)


def local(
    text_states,
    image_states,
    image_start,
    w_query,
    w_key,
    w_value,
    w_out,
    query_gain,
    key_gain,
    cross_gate,
):
    sections = lax.axis_size("pipe")
    section_index = lax.axis_index("pipe")
    head_size = w_key.shape[2]
    weights = gathered_rows(jnp.concatenate([w_key[0], w_value[0]], axis=1))
    pictures = column_slices(image_states)
    parts, depth = lax.axis_size("x"), weights.shape[0]
    sums = jnp.dot(pictures.reshape(-1, depth), weights, preferred_element_type=jnp.float32)
    sums = sums.reshape(pictures.shape[:-1] + (2 * head_size,))
    own = lax.axis_index("x")
    total = lax.dynamic_index_in_dim(sums, own, 1, keepdims=False)
    rounded = sums.astype(jnp.bfloat16)
    for distance in range(1, parts):
        block = lax.dynamic_index_in_dim(rounded, own ^ distance, 1, keepdims=False)
        total = total + exchanged(block, "x", distance).astype(jnp.float32)
    total = jnp.swapaxes(total, 0, 1)
    total = total.reshape(total.shape[0], -1, 2 * head_size)
    key_rows = normalized(total[..., :head_size], key_gain[0]).astype(jnp.bfloat16)
    value_rows = total[..., head_size:].astype(jnp.bfloat16)
    factor = jnp.tanh(cross_gate)
    current = text_states[0]
    for moment in range(sections):
        holding = jnp.mod(section_index - moment, sections)
        active = (moment <= section_index).astype(jnp.int32)
        current = layer(
            jnp.stack([holding, active]),
            image_start[:, 0],
            factor,
            current,
            key_rows,
            value_rows,
            query_gain,
            w_query[0],
            w_out[0],
        )
        current = shifted(current, "pipe", 1)
    return current[None]


def solution(mesh):
    sections = mesh.shape["pipe"]
    planes, far = 4, 2
    groups = mesh.shape["dp"] // (planes * far)
    mesh = Mesh(mesh.devices.reshape(planes, groups, far, sections), ("x", "z", "yh", "pipe"))
    replicas = ("x", "z", "yh")
    placed = (
        P("pipe", replicas, None),
        P(None, replicas + ("pipe",), None),
        P(None, replicas),
        P("pipe", None, None),
        P("pipe", replicas, None),
        P("pipe", replicas, None),
        P("pipe", None, None),
        P("pipe", None),
        P("pipe", None),
        P("pipe"),
    )
    return jax.shard_map(
        local, mesh=mesh, in_specs=placed, out_specs=P("pipe", replicas, None), check_vma=False
    )
```

```python
import functools
import math

import jax
import jax.numpy as jnp
from jax import lax
from jax.experimental import pallas as pl
from jax.experimental.pallas import tpu as pltpu
from jax.sharding import Mesh
from jax.sharding import PartitionSpec as P

epsilon = 1e-06
VMEM_LIMIT = 60 * 2**20


def unit(projected):
    mean_square = jnp.mean(projected * projected, axis=-1, keepdims=True)
    return projected * lax.rsqrt(mean_square + epsilon)


def layer_kernel(
    parts,
    arrivals,
    choosing,
    choice_ref,
    first_seen_ref,
    *refs,
):
    states = refs[:arrivals]
    (
        own_rows_ref,
        near_rows_ref,
        own_query_ref,
        near_query_ref,
        own_out_ref,
        near_out_ref,
        out_ref,
        query_weight,
        out_weight,
        sems,
    ) = refs[arrivals:]
    rows, width = out_ref.shape
    columns = query_weight.shape[1]
    head_size = own_rows_ref.shape[2] // 2
    heads = columns // head_size
    step = width // parts
    active = choice_ref[0] == 1
    near = choice_ref[1] == 1
    batch = choice_ref[2]

    def piece(part):
        return pl.ds(part * step, step)

    def query_copy(ref, part):
        return pltpu.make_async_copy(
            ref.at[piece(part), :], query_weight.at[piece(part), :], sems.at[0, part]
        )

    def out_copy(ref, part):
        return pltpu.make_async_copy(
            ref.at[:, piece(part)], out_weight.at[:, piece(part)], sems.at[1, part]
        )

    def state(part):
        held = states[0][:, piece(part)]
        for index in range(1, choosing):
            held = jnp.where(choice_ref[4] == index, states[index][:, piece(part)], held)
        return held

    @pl.when(jnp.logical_and(active, near))
    def _():
        for part in range(parts):
            query_copy(near_query_ref, part).start()
        for part in range(parts):
            out_copy(near_out_ref, part).start()

    @pl.when(jnp.logical_and(active, jnp.logical_not(near)))
    def _():
        for part in range(parts):
            query_copy(own_query_ref, part).start()
        for part in range(parts):
            out_copy(own_out_ref, part).start()

    @pl.when(active)
    def _():
        query_sums = jnp.zeros((rows, columns), jnp.float32)
        for part in range(parts):
            query_copy(own_query_ref, part).wait()
            query_sums += jnp.dot(
                state(part), query_weight[piece(part), :], preferred_element_type=jnp.float32
            )
        stacked = jnp.concatenate(
            [query_sums[:, h * head_size : (h + 1) * head_size] for h in range(heads)], axis=0
        )
        queries = unit(stacked).astype(jnp.bfloat16)
        image_rows = jnp.where(near, near_rows_ref[choice_ref[3]], own_rows_ref[batch])
        scores = lax.dot_general(
            queries,
            image_rows[:, :head_size],
            (((1,), (1,)), ((), ())),
            preferred_element_type=jnp.float32,
        ) / math.sqrt(head_size)
        exponent = jnp.exp(scores)
        probs = (exponent / jnp.sum(exponent, axis=-1, keepdims=True)).astype(jnp.bfloat16)
        attended = jnp.dot(probs, image_rows[:, head_size:], preferred_element_type=jnp.float32)
        attended = attended.astype(jnp.bfloat16)
        attended = jnp.concatenate(
            [attended[h * rows : (h + 1) * rows] for h in range(heads)], axis=1
        )
        positions = lax.broadcasted_iota(jnp.int32, (rows, 1), 0)
        seen = (positions >= first_seen_ref[batch]).astype(jnp.float32)
        for part in range(parts):
            out_copy(own_out_ref, part).wait()
            update = jnp.dot(attended, out_weight[:, piece(part)], preferred_element_type=jnp.float32)
            result = state(part).astype(jnp.float32) + seen * update
            out_ref[:, piece(part)] = result.astype(jnp.bfloat16)

    for index in range(arrivals):

        @pl.when(jnp.logical_and(jnp.logical_not(active), choice_ref[4] == index))
        def _(index=index):
            out_ref[...] = states[index][...]


def layer(choice, first_seen, states, own_rows, near_rows, weights, choosing=1):
    parts = 4
    rows, width = states[0].shape
    columns = weights[0].shape[1]
    smem = pl.BlockSpec(memory_space=pltpu.SMEM)
    vmem = pl.BlockSpec(memory_space=pltpu.VMEM)
    return pl.pallas_call(
        functools.partial(layer_kernel, parts, len(states), choosing),
        out_shape=jax.ShapeDtypeStruct((rows, width), states[0].dtype),
        in_specs=[smem] * 2
        + [vmem] * (len(states) + 2)
        + [pl.BlockSpec(memory_space=pl.ANY)] * 4,
        out_specs=vmem,
        scratch_shapes=[
            pltpu.VMEM((width, columns), jnp.bfloat16),
            pltpu.VMEM((columns, width), jnp.bfloat16),
            pltpu.SemaphoreType.DMA((2, parts)),
        ],
        compiler_params=pltpu.CompilerParams(vmem_limit_bytes=VMEM_LIMIT),
        cost_estimate=pl.CostEstimate(
            flops=4 * rows * width * columns,
            bytes_accessed=4 * width * columns,
            transcendentals=rows * columns,
        ),
    )(jnp.stack(choice).astype(jnp.int32), first_seen, *states, own_rows, near_rows, *weights)


def exchanged(block, axis, distance):
    devices = range(lax.axis_size(axis))
    return lax.ppermute(block, axis, [(i, i ^ distance) for i in devices])


def doubled(known, axis, distance, where):
    other = exchanged(known, axis, distance)
    upper = (lax.axis_index(axis) & distance) != 0
    first = jnp.where(upper, other, known)
    second = jnp.where(upper, known, other)
    return jnp.stack([first, second], axis=where)


def joined(known, axis, distance):
    known = doubled(known, axis, distance, 1)
    return known if axis == "yh" else known.reshape((-1,) + known.shape[2:])


def column_slices(image_states):
    batches, rows, width = image_states.shape
    parts = lax.axis_size("x")
    own = lax.axis_index("x")
    depth = width // parts

    def columns(plane):
        return lax.dynamic_slice_in_dim(image_states, plane * depth, depth, 2)

    blocks = [columns(own)]
    for distance in range(1, parts):
        blocks.append(exchanged(columns(own ^ distance), "x", distance))
    ordered = jnp.stack(blocks)
    ordered = jnp.take(ordered, own ^ jnp.arange(parts), axis=0)
    halves = doubled(ordered, "pipe", 2, 0)
    return doubled(halves, "pipe", 1, 1).reshape((-1,) + ordered.shape)


def local(
    text_states,
    image_states,
    image_start,
    w_query,
    w_key,
    w_value,
    w_out,
    query_gain,
    key_gain,
    cross_gate,
):
    sections = lax.axis_size("pipe")
    section_index = lax.axis_index("pipe")
    head_size = w_key.shape[2]
    known = jnp.concatenate([w_key[0], w_value[0]], axis=1)[None]
    known = joined(known, "yh", 1)
    distance = lax.axis_size("z") // 2
    known = joined(known, "z", distance)
    known, image_states = lax.optimization_barrier((known, image_states))
    pictures = column_slices(image_states)
    distance //= 2
    known = joined(known, "z", distance)
    known, w_query, w_out = lax.optimization_barrier((known, w_query, w_out))
    layer_weights = (
        w_query[0],
        exchanged(w_query[0], "pipe", 1),
        w_out[0],
        exchanged(w_out[0], "pipe", 1),
    )
    while distance > 1:
        distance //= 2
        known = joined(known, "z", distance)
    weights = known.reshape(-1, known.shape[-1])
    parts, depth = lax.axis_size("x"), weights.shape[0]
    sums = jnp.dot(pictures.reshape(-1, depth), weights, preferred_element_type=jnp.float32)
    sums = sums.reshape(pictures.shape[:-1] + (2 * head_size,))
    own = lax.axis_index("x")
    total = lax.dynamic_index_in_dim(sums, own, 1, keepdims=False)
    rounded = sums.astype(jnp.bfloat16)
    for distance in range(1, parts):
        block = lax.dynamic_index_in_dim(rounded, own ^ distance, 1, keepdims=False)
        total = total + exchanged(block, "x", distance).astype(jnp.float32)
    total = jnp.swapaxes(total, 0, 1)
    total = total.reshape(total.shape[0], -1, 2 * head_size)
    key_scale = key_gain * query_gain
    key_rows = (unit(total[..., :head_size]) * key_scale[0]).astype(jnp.bfloat16)
    value_rows = (total[..., head_size:] * jnp.tanh(cross_gate[0])).astype(jnp.bfloat16)
    own_rows = jnp.concatenate([key_rows, value_rows], axis=-1)
    parity = section_index & 1
    later_half = section_index >= sections // 2
    by_parity = own_rows.reshape((sections // 2, 2) + own_rows.shape[1:])
    near_rows = exchanged(
        lax.dynamic_index_in_dim(by_parity, 1 - parity, 1, keepdims=False), "pipe", 1
    )
    always, never = jnp.int32(1), jnp.int32(0)
    own_batch = section_index
    own_weights = (w_query[0], w_query[0], w_out[0], w_out[0])
    first = layer(
        (always, never, own_batch, never, never),
        image_start[:, 0],
        (text_states[0],),
        own_rows,
        own_rows,
        own_weights,
    )
    run = functools.partial(
        layer,
        first_seen=image_start[:, 0],
        own_rows=own_rows,
        near_rows=near_rows,
        weights=layer_weights,
    )
    from_odd = lax.ppermute(first, "pipe", [(1, 3)])
    second = run((1 - parity, always, own_batch, own_batch >> 1, never), states=(first,))
    from_even = lax.ppermute(second, "pipe", [(0, 2)])
    even = (section_index == 2).astype(jnp.int32)
    odd = (section_index == 3).astype(jnp.int32)
    late = later_half.astype(jnp.int32)
    ahead = run((odd, always, odd, never, never), states=(from_odd,))
    third = run((late, never, odd, never, odd), states=(from_even, ahead), choosing=2)
    home_odd = lax.ppermute(third, "pipe", [(3, 1)])
    kept = jnp.where(section_index == 1, 1, 2 * odd)
    fourth = run((even, always, never, never, kept), states=(third, home_odd, second), choosing=1)
    home_even = lax.ppermute(fourth, "pipe", [(2, 0)])
    kept_state = jnp.where(section_index == 2, second, fourth)
    return jnp.where(section_index == 0, home_even, kept_state)[None]


def solution(mesh):
    sections = mesh.shape["pipe"]
    planes, far = 4, 2
    groups = mesh.shape["dp"] // (planes * far)
    mesh = Mesh(mesh.devices.reshape(planes, groups, far, sections), ("x", "z", "yh", "pipe"))
    replicas = ("x", "z", "yh")
    placed = (
        P("pipe", replicas, None),
        P(None, replicas + ("pipe",), None),
        P(None, replicas),
        P("pipe", None, None),
        P("pipe", replicas, None),
        P("pipe", replicas, None),
        P("pipe", None, None),
        P("pipe", None),
        P("pipe", None),
        P("pipe"),
    )
    return jax.shard_map(
        local, mesh=mesh, in_specs=placed, out_specs=P("pipe", replicas, None), check_vma=False
    )
```

```python
import functools
import math

import jax
import jax.numpy as jnp
from jax import lax
from jax.experimental import pallas as pl
from jax.experimental.pallas import tpu as pltpu
from jax.sharding import Mesh
from jax.sharding import PartitionSpec as P

epsilon = 1e-06
VMEM_LIMIT = 48 * 2**20
SECTIONS = 4


def unit(projected):
    mean_square = jnp.mean(projected * projected, axis=-1, keepdims=True)
    return projected * lax.rsqrt(mean_square + epsilon)


def layer_kernel(slot, arrivals, choosing, section_ref, first_seen_ref, *refs):
    states = refs[:arrivals]
    rows_ref, weights_ref, out_ref, weights, sems = refs[arrivals:]
    rows, width = out_ref.shape
    columns = weights.shape[1]
    head_size = rows_ref.shape[2] // 2
    heads = columns // head_size
    pieces = sems.shape[0]
    depth = weights.shape[0] // pieces
    active, batch, chosen = slot(section_ref[0])

    def fetch(piece):
        rows_of = pl.ds(piece * depth, depth)
        return pltpu.make_async_copy(weights_ref.at[rows_of, :], weights.at[rows_of, :], sems.at[piece])

    def state(start, size):
        held = states[0][:, start : start + size]
        for index in range(1, choosing):
            held = jnp.where(chosen == index, states[index][:, start : start + size], held)
        return held

    @pl.when(active)
    def _():
        for piece in range(pieces):
            fetch(piece).start()
        query_sums = jnp.zeros((rows, columns), jnp.float32)
        for piece in range(width // depth):
            fetch(piece).wait()
            start = piece * depth
            query_sums += jnp.dot(
                state(start, depth), weights[start : start + depth], preferred_element_type=jnp.float32
            )
        stacked = jnp.concatenate(
            [query_sums[:, h * head_size : (h + 1) * head_size] for h in range(heads)], axis=0
        )
        queries = unit(stacked).astype(jnp.bfloat16)
        image_rows = rows_ref[batch if rows_ref.shape[0] == SECTIONS else batch >> 1]
        scores = lax.dot_general(
            queries,
            image_rows[:, :head_size],
            (((1,), (1,)), ((), ())),
            preferred_element_type=jnp.float32,
        ) / math.sqrt(head_size)
        exponent = jnp.exp(scores)
        probs = (exponent / jnp.sum(exponent, axis=-1, keepdims=True)).astype(jnp.bfloat16)
        attended = jnp.dot(probs, image_rows[:, head_size:], preferred_element_type=jnp.float32)
        attended = attended.astype(jnp.bfloat16)
        attended = jnp.concatenate(
            [attended[h * rows : (h + 1) * rows] for h in range(heads)], axis=1
        )
        positions = lax.broadcasted_iota(jnp.int32, (rows, 1), 0)
        seen = (positions >= first_seen_ref[batch]).astype(jnp.float32)
        for start in range(0, width, columns):
            if start % depth == 0:
                fetch((width + start) // depth).wait()
            block = weights[width + start : width + start + columns]
            update = jnp.dot(attended, block, preferred_element_type=jnp.float32)
            result = state(start, columns).astype(jnp.float32) + seen * update
            out_ref[:, start : start + columns] = result.astype(jnp.bfloat16)

    for index in range(arrivals):

        @pl.when(jnp.logical_and(jnp.logical_not(active), chosen == index))
        def _(index=index):
            out_ref[...] = states[index][...]


def stack_kernel(w_query_ref, w_out_ref, out_ref, sems):
    width, columns = w_query_ref.shape
    copies = [pltpu.make_async_copy(w_query_ref, out_ref.at[pl.ds(0, width), :], sems.at[0])]
    for block in range(width // columns):
        copies.append(
            pltpu.make_async_copy(
                w_out_ref.at[:, pl.ds(block * columns, columns)],
                out_ref.at[pl.ds(width + block * columns, columns), :],
                sems.at[1 + block],
            )
        )
    for copy in copies:
        copy.start()
    for copy in copies:
        copy.wait()


def stacked_weights(w_query, w_out):
    width, columns = w_query.shape
    return pl.pallas_call(
        stack_kernel,
        out_shape=jax.ShapeDtypeStruct((2 * width, columns), w_query.dtype),
        in_specs=[pl.BlockSpec(memory_space=pl.ANY)] * 2,
        out_specs=pl.BlockSpec(memory_space=pl.ANY),
        scratch_shapes=[pltpu.SemaphoreType.DMA((1 + width // columns,))],
        compiler_params=pltpu.CompilerParams(vmem_limit_bytes=VMEM_LIMIT),
        cost_estimate=pl.CostEstimate(
            flops=0, bytes_accessed=8 * width * columns, transcendentals=0
        ),
    )(w_query, w_out)


def slot_own(section):
    return section >= 0, section, 0


def slot_second(section):
    return (section & 1) == 0, section, 0


def slot_ahead(section):
    return section == 3, jnp.int32(1), 0


def slot_third(section):
    odd = jnp.where(section == 3, 1, 0)
    return section >= 2, odd, odd


def slot_fourth(section):
    kept = jnp.where(section == 1, 1, jnp.where(section == 3, 2, 0))
    return section == 2, jnp.int32(0), kept


def layer(slot, section, first_seen, states, rows_by_batch, weights, choosing=1):
    rows, width = states[0].shape
    columns = weights.shape[1]
    smem = pl.BlockSpec(memory_space=pltpu.SMEM)
    vmem = pl.BlockSpec(memory_space=pltpu.VMEM)
    return pl.pallas_call(
        functools.partial(layer_kernel, slot, len(states), choosing),
        out_shape=jax.ShapeDtypeStruct((rows, width), states[0].dtype),
        in_specs=[smem] * 2
        + [vmem] * (len(states) + 1)
        + [pl.BlockSpec(memory_space=pl.ANY)],
        out_specs=vmem,
        scratch_shapes=[
            pltpu.VMEM(weights.shape, weights.dtype),
            pltpu.SemaphoreType.DMA((2 * max(1, width // (2 * columns)),)),
        ],
        compiler_params=pltpu.CompilerParams(vmem_limit_bytes=VMEM_LIMIT),
        cost_estimate=pl.CostEstimate(
            flops=4 * rows * width * columns,
            bytes_accessed=4 * width * columns,
            transcendentals=rows * columns,
        ),
    )(section, first_seen, *states, rows_by_batch, weights)


def exchanged(block, axis, distance):
    devices = range(lax.axis_size(axis))
    return lax.ppermute(block, axis, [(i, i ^ distance) for i in devices])


def doubled(known, axis, distance, where):
    other = exchanged(known, axis, distance)
    upper = (lax.axis_index(axis) & distance) != 0
    first = jnp.where(upper, other, known)
    second = jnp.where(upper, known, other)
    return jnp.stack([first, second], axis=where)


def joined(known, axis, distance):
    known = doubled(known, axis, distance, 1)
    return known if axis == "yh" else known.reshape((-1,) + known.shape[2:])


def column_slices(image_states):
    batches, rows, width = image_states.shape
    parts = lax.axis_size("x")
    own = lax.axis_index("x")
    depth = width // parts

    def columns(plane):
        return lax.dynamic_slice_in_dim(image_states, plane * depth, depth, 2)

    blocks = [columns(own)]
    for distance in range(1, parts):
        blocks.append(exchanged(columns(own ^ distance), "x", distance))
    ordered = jnp.stack(blocks)
    ordered = jnp.take(ordered, own ^ jnp.arange(parts), axis=0)
    halves = doubled(ordered, "pipe", 2, 0)
    return doubled(halves, "pipe", 1, 1).reshape((-1,) + ordered.shape)


def local(
    text_states,
    image_states,
    image_start,
    w_query,
    w_key,
    w_value,
    w_out,
    query_gain,
    key_gain,
    cross_gate,
):
    sections = lax.axis_size("pipe")
    section_index = lax.axis_index("pipe")
    head_size = w_key.shape[2]
    known = jnp.concatenate([w_key[0], w_value[0]], axis=1)[None]
    known = joined(known, "yh", 1)
    distance = lax.axis_size("z") // 2
    known = joined(known, "z", distance)
    known, image_states = lax.optimization_barrier((known, image_states))
    pictures = column_slices(image_states)
    distance //= 2
    known = joined(known, "z", distance)
    own_weights = stacked_weights(w_query[0], w_out[0])
    known, own_weights = lax.optimization_barrier((known, own_weights))
    near_weights = exchanged(own_weights, "pipe", 1)
    while distance > 1:
        distance //= 2
        known = joined(known, "z", distance)
    weights = known.reshape(-1, known.shape[-1])
    parts, depth = lax.axis_size("x"), weights.shape[0]
    sums = jnp.dot(pictures.reshape(-1, depth), weights, preferred_element_type=jnp.float32)
    sums = sums.reshape(pictures.shape[:-1] + (2 * head_size,))
    own = lax.axis_index("x")
    total = lax.dynamic_index_in_dim(sums, own, 1, keepdims=False)
    rounded = sums.astype(jnp.bfloat16)
    for distance in range(1, parts):
        block = lax.dynamic_index_in_dim(rounded, own ^ distance, 1, keepdims=False)
        total = total + exchanged(block, "x", distance).astype(jnp.float32)
    total = jnp.swapaxes(total, 0, 1)
    total = total.reshape(total.shape[0], -1, 2 * head_size)
    key_scale = key_gain * query_gain
    key_rows = (unit(total[..., :head_size]) * key_scale[0]).astype(jnp.bfloat16)
    value_rows = (total[..., head_size:] * jnp.tanh(cross_gate[0])).astype(jnp.bfloat16)
    own_rows = jnp.concatenate([key_rows, value_rows], axis=-1)
    parity = section_index & 1
    by_parity = own_rows.reshape((sections // 2, 2) + own_rows.shape[1:])
    near_rows = exchanged(
        lax.dynamic_index_in_dim(by_parity, 1 - parity, 1, keepdims=False), "pipe", 1
    )
    section = section_index[None]
    first_seen = image_start[:, 0]
    run = functools.partial(layer, section=section, first_seen=first_seen)
    own = dict(rows_by_batch=own_rows, weights=own_weights)
    near = dict(rows_by_batch=near_rows, weights=near_weights)
    first = run(slot_own, states=(text_states[0],), **own)
    from_odd = lax.ppermute(first, "pipe", [(1, 3)])
    second = run(slot_second, states=(first,), **near)
    from_even = lax.ppermute(second, "pipe", [(0, 2)])
    ahead = run(slot_ahead, states=(from_odd,), **near)
    third = run(slot_third, states=(from_even, ahead), choosing=2, **own)
    home_odd = lax.ppermute(third, "pipe", [(3, 1)])
    fourth = run(slot_fourth, states=(third, home_odd, second), **near)
    home_even = lax.ppermute(fourth, "pipe", [(2, 0)])
    kept_state = jnp.where(section_index == 2, second, fourth)
    return jnp.where(section_index == 0, home_even, kept_state)[None]


def solution(mesh):
    sections = mesh.shape["pipe"]
    planes, far = 4, 2
    groups = mesh.shape["dp"] // (planes * far)
    mesh = Mesh(mesh.devices.reshape(planes, groups, far, sections), ("x", "z", "yh", "pipe"))
    replicas = ("x", "z", "yh")
    placed = (
        P("pipe", replicas, None),
        P(None, replicas + ("pipe",), None),
        P(None, replicas),
        P("pipe", None, None),
        P("pipe", replicas, None),
        P("pipe", replicas, None),
        P("pipe", None, None),
        P("pipe", None),
        P("pipe", None),
        P("pipe"),
    )
    return jax.shard_map(
        local, mesh=mesh, in_specs=placed, out_specs=P("pipe", replicas, None), check_vma=False
    )
```

```python
import functools
import math

import jax
import jax.numpy as jnp
from jax import lax
from jax.experimental import pallas as pl
from jax.experimental.pallas import tpu as pltpu
from jax.sharding import Mesh
from jax.sharding import PartitionSpec as P

epsilon = 1e-06
VMEM_LIMIT = 48 * 2**20
SECTIONS = 4


def unit(projected):
    mean_square = jnp.mean(projected * projected, axis=-1, keepdims=True)
    return projected * lax.rsqrt(mean_square + epsilon)


def layer_kernel(slot, arrivals, choosing, section_ref, first_seen_ref, *refs):
    states = refs[:arrivals]
    rows_ref, weights_ref, out_ref, weights, sems = refs[arrivals:]
    rows, width = out_ref.shape
    columns = weights.shape[1]
    head_size = rows_ref.shape[2] // 2
    heads = columns // head_size
    pieces = sems.shape[0]
    depth = weights.shape[0] // pieces
    active, batch, chosen = slot(section_ref[0])

    def fetch(piece):
        rows_of = pl.ds(piece * depth, depth)
        return pltpu.make_async_copy(weights_ref.at[rows_of, :], weights.at[rows_of, :], sems.at[piece])

    def state(start, size):
        held = states[0][:, start : start + size]
        for index in range(1, choosing):
            held = jnp.where(chosen == index, states[index][:, start : start + size], held)
        return held

    @pl.when(active)
    def _():
        for piece in range(pieces):
            fetch(piece).start()
        query_sums = jnp.zeros((rows, columns), jnp.float32)
        for piece in range(width // depth):
            fetch(piece).wait()
            start = piece * depth
            query_sums += jnp.dot(
                state(start, depth), weights[start : start + depth], preferred_element_type=jnp.float32
            )
        stacked = jnp.concatenate(
            [query_sums[:, h * head_size : (h + 1) * head_size] for h in range(heads)], axis=0
        )
        queries = unit(stacked).astype(jnp.bfloat16)
        image_rows = rows_ref[batch if rows_ref.shape[0] == SECTIONS else batch >> 1]
        scores = lax.dot_general(
            queries,
            image_rows[:, :head_size],
            (((1,), (1,)), ((), ())),
            preferred_element_type=jnp.float32,
        ) / math.sqrt(head_size)
        exponent = jnp.exp(scores)
        probs = (exponent / jnp.sum(exponent, axis=-1, keepdims=True)).astype(jnp.bfloat16)
        attended = jnp.dot(probs, image_rows[:, head_size:], preferred_element_type=jnp.float32)
        attended = attended.astype(jnp.bfloat16)
        attended = jnp.concatenate(
            [attended[h * rows : (h + 1) * rows] for h in range(heads)], axis=1
        )
        positions = lax.broadcasted_iota(jnp.int32, (rows, 1), 0)
        seen = (positions >= first_seen_ref[batch]).astype(jnp.float32)
        for start in range(0, width, columns):
            if start % depth == 0:
                fetch((width + start) // depth).wait()
            block = weights[width + start : width + start + columns]
            update = jnp.dot(attended, block, preferred_element_type=jnp.float32)
            result = state(start, columns).astype(jnp.float32) + seen * update
            out_ref[:, start : start + columns] = result.astype(jnp.bfloat16)

    for index in range(arrivals):

        @pl.when(jnp.logical_and(jnp.logical_not(active), chosen == index))
        def _(index=index):
            out_ref[...] = states[index][...]


def stack_kernel(w_query_ref, w_out_ref, out_ref, held, in_sems, out_sems):
    width, columns = w_query_ref.shape
    pieces = in_sems.shape[0]
    arriving, leaving = [], []
    for piece in range(pieces):
        rows = pl.ds(piece * columns, columns)
        below = piece * columns - width
        if below < 0:
            source = w_query_ref.at[rows, :]
        else:
            source = w_out_ref.at[:, pl.ds(below, columns)]
        arriving.append(pltpu.make_async_copy(source, held.at[rows, :], in_sems.at[piece]))
        leaving.append(pltpu.make_async_copy(held.at[rows, :], out_ref.at[rows, :], out_sems.at[piece]))
    for copy in arriving:
        copy.start()
    for piece in range(pieces):
        arriving[piece].wait()
        leaving[piece].start()
    for copy in leaving:
        copy.wait()


def stacked_weights(w_query, w_out):
    width, columns = w_query.shape
    return pl.pallas_call(
        stack_kernel,
        out_shape=jax.ShapeDtypeStruct((2 * width, columns), w_query.dtype),
        in_specs=[pl.BlockSpec(memory_space=pl.ANY)] * 2,
        out_specs=pl.BlockSpec(memory_space=pl.ANY),
        scratch_shapes=[
            pltpu.VMEM((2 * width, columns), w_query.dtype),
            pltpu.SemaphoreType.DMA((2 * width // columns,)),
            pltpu.SemaphoreType.DMA((2 * width // columns,)),
        ],
        compiler_params=pltpu.CompilerParams(vmem_limit_bytes=VMEM_LIMIT),
        cost_estimate=pl.CostEstimate(
            flops=0, bytes_accessed=8 * width * columns, transcendentals=0
        ),
    )(w_query, w_out)


def slot_own(section):
    return section >= 0, section, 0


def slot_second(section):
    return (section & 1) == 0, section, 0


def slot_ahead(section):
    return section == 3, jnp.int32(1), 0


def slot_third(section):
    odd = jnp.where(section == 3, 1, 0)
    return section >= 2, odd, odd


def slot_fourth(section):
    kept = jnp.where(section == 1, 1, jnp.where(section == 3, 2, 0))
    return section == 2, jnp.int32(0), kept


def layer(slot, section, first_seen, states, rows_by_batch, weights, choosing=1):
    rows, width = states[0].shape
    columns = weights.shape[1]
    smem = pl.BlockSpec(memory_space=pltpu.SMEM)
    vmem = pl.BlockSpec(memory_space=pltpu.VMEM)
    return pl.pallas_call(
        functools.partial(layer_kernel, slot, len(states), choosing),
        out_shape=jax.ShapeDtypeStruct((rows, width), states[0].dtype),
        in_specs=[smem] * 2
        + [vmem] * (len(states) + 1)
        + [pl.BlockSpec(memory_space=pl.ANY)],
        out_specs=vmem,
        scratch_shapes=[
            pltpu.VMEM(weights.shape, weights.dtype),
            pltpu.SemaphoreType.DMA((2 * max(1, width // (2 * columns)),)),
        ],
        compiler_params=pltpu.CompilerParams(vmem_limit_bytes=VMEM_LIMIT),
        cost_estimate=pl.CostEstimate(
            flops=4 * rows * width * columns,
            bytes_accessed=4 * width * columns,
            transcendentals=rows * columns,
        ),
    )(section, first_seen, *states, rows_by_batch, weights)


def exchanged(block, axis, distance):
    devices = range(lax.axis_size(axis))
    return lax.ppermute(block, axis, [(i, i ^ distance) for i in devices])


def doubled(known, axis, distance, where):
    other = exchanged(known, axis, distance)
    upper = (lax.axis_index(axis) & distance) != 0
    first = jnp.where(upper, other, known)
    second = jnp.where(upper, known, other)
    return jnp.stack([first, second], axis=where)


def joined(known, axis, distance):
    known = doubled(known, axis, distance, 1)
    return known if axis == "yh" else known.reshape((-1,) + known.shape[2:])


def in_order(own, blocks):
    low, high = (own & 1) != 0, (own & 2) != 0
    near = [jnp.where(low, blocks[1], blocks[0]), jnp.where(low, blocks[0], blocks[1])]
    far = [jnp.where(low, blocks[3], blocks[2]), jnp.where(low, blocks[2], blocks[3])]
    first = [jnp.where(high, f, n) for n, f in zip(near, far)]
    second = [jnp.where(high, n, f) for n, f in zip(near, far)]
    return jnp.stack(first + second)


def joined_four(known, distance):
    blocks = {0: known}
    for step in (2, 1, 3):
        blocks[step] = exchanged(known, "z", step * distance)
    own = (lax.axis_index("z") // distance) & 3
    ordered = in_order(own, blocks)
    return ordered.reshape((-1,) + known.shape[1:])


def column_slices(image_states):
    width = image_states.shape[2]
    parts = lax.axis_size("x")
    own = lax.axis_index("x")
    depth = width // parts

    def columns(plane):
        return lax.dynamic_slice_in_dim(image_states, plane * depth, depth, 2)

    blocks = [columns(own)]
    for distance in range(1, parts):
        blocks.append(exchanged(columns(own ^ distance), "x", distance))
    return blocks


def local(
    text_states,
    image_states,
    image_start,
    w_query,
    w_key,
    w_value,
    w_out,
    query_gain,
    key_gain,
    cross_gate,
):
    sections = lax.axis_size("pipe")
    section_index = lax.axis_index("pipe")
    head_size = w_key.shape[2]
    known = jnp.concatenate([w_key[0], w_value[0]], axis=1)[None]
    known = joined(known, "yh", 1)
    known, image_states, w_query, w_out = lax.optimization_barrier(
        (known, image_states, w_query, w_out)
    )
    distance = lax.axis_size("z") // 4
    known = joined_four(known, distance)
    slices = column_slices(image_states)
    own_weights = stacked_weights(w_query[0], w_out[0])
    known, slices, own_weights = lax.optimization_barrier((known, slices, own_weights))
    ordered = in_order(lax.axis_index("x"), slices)
    halves = doubled(ordered, "pipe", 2, 0)
    distance //= 2
    known = joined(known, "z", distance)
    known, halves, own_weights = lax.optimization_barrier((known, halves, own_weights))
    pictures = doubled(halves, "pipe", 1, 1).reshape((-1,) + ordered.shape)
    near_weights = exchanged(own_weights, "pipe", 1)
    while distance > 1:
        distance //= 2
        known = joined(known, "z", distance)
    weights = known.reshape(-1, known.shape[-1])
    parts, depth = lax.axis_size("x"), weights.shape[0]
    sums = jnp.dot(pictures.reshape(-1, depth), weights, preferred_element_type=jnp.float32)
    sums = sums.reshape(pictures.shape[:-1] + (2 * head_size,))
    own = lax.axis_index("x")
    total = lax.dynamic_index_in_dim(sums, own, 1, keepdims=False)
    rounded = sums.astype(jnp.bfloat16)
    for distance in range(1, parts):
        block = lax.dynamic_index_in_dim(rounded, own ^ distance, 1, keepdims=False)
        total = total + exchanged(block, "x", distance).astype(jnp.float32)
    total = jnp.swapaxes(total, 0, 1)
    total = total.reshape(total.shape[0], -1, 2 * head_size)
    key_scale = key_gain * query_gain
    key_rows = (unit(total[..., :head_size]) * key_scale[0]).astype(jnp.bfloat16)
    value_rows = (total[..., head_size:] * jnp.tanh(cross_gate[0])).astype(jnp.bfloat16)
    own_rows = jnp.concatenate([key_rows, value_rows], axis=-1)
    parity = section_index & 1
    by_parity = own_rows.reshape((sections // 2, 2) + own_rows.shape[1:])
    near_rows = exchanged(
        lax.dynamic_index_in_dim(by_parity, 1 - parity, 1, keepdims=False), "pipe", 1
    )
    section = section_index[None]
    first_seen = image_start[:, 0]
    run = functools.partial(layer, section=section, first_seen=first_seen)
    own = dict(rows_by_batch=own_rows, weights=own_weights)
    near = dict(rows_by_batch=near_rows, weights=near_weights)
    first = run(slot_own, states=(text_states[0],), **own)
    from_odd = lax.ppermute(first, "pipe", [(1, 3)])
    second = run(slot_second, states=(first,), **near)
    from_even = lax.ppermute(second, "pipe", [(0, 2)])
    ahead = run(slot_ahead, states=(from_odd,), **near)
    third = run(slot_third, states=(from_even, ahead), choosing=2, **own)
    home_odd = lax.ppermute(third, "pipe", [(3, 1)])
    fourth = run(slot_fourth, states=(third, home_odd, second), **near)
    home_even = lax.ppermute(fourth, "pipe", [(2, 0)])
    kept_state = jnp.where(section_index == 2, second, fourth)
    return jnp.where(section_index == 0, home_even, kept_state)[None]


def solution(mesh):
    sections = mesh.shape["pipe"]
    planes, far = 4, 2
    groups = mesh.shape["dp"] // (planes * far)
    mesh = Mesh(mesh.devices.reshape(planes, groups, far, sections), ("x", "z", "yh", "pipe"))
    replicas = ("x", "z", "yh")
    placed = (
        P("pipe", replicas, None),
        P(None, replicas + ("pipe",), None),
        P(None, replicas),
        P("pipe", None, None),
        P("pipe", replicas, None),
        P("pipe", replicas, None),
        P("pipe", None, None),
        P("pipe", None),
        P("pipe", None),
        P("pipe"),
    )
    return jax.shard_map(
        local, mesh=mesh, in_specs=placed, out_specs=P("pipe", replicas, None), check_vma=False
    )
```

```python
import functools
import math

import jax
import jax.numpy as jnp
from jax import lax
from jax.experimental import pallas as pl
from jax.experimental.pallas import tpu as pltpu
from jax.sharding import Mesh
from jax.sharding import PartitionSpec as P

epsilon = 1e-06
VMEM_LIMIT = 48 * 2**20
SECTIONS = 4


def unit(projected):
    mean_square = jnp.mean(projected * projected, axis=-1, keepdims=True)
    return projected * lax.rsqrt(mean_square + epsilon)


def layer_kernel(slot, arrivals, choosing, section_ref, first_seen_ref, *refs):
    states = refs[:arrivals]
    rows_ref, weights_ref, out_ref, weights, sems = refs[arrivals:]
    rows, width = out_ref.shape
    columns = weights.shape[1]
    head_size = rows_ref.shape[2] // 2
    heads = columns // head_size
    pieces = sems.shape[0]
    depth = weights.shape[0] // pieces
    active, batch, chosen = slot(section_ref[0])

    def fetch(piece):
        rows_of = pl.ds(piece * depth, depth)
        return pltpu.make_async_copy(weights_ref.at[rows_of, :], weights.at[rows_of, :], sems.at[piece])

    def state(start, size):
        held = states[0][:, start : start + size]
        for index in range(1, choosing):
            held = jnp.where(chosen == index, states[index][:, start : start + size], held)
        return held

    @pl.when(active)
    def _():
        for piece in range(pieces):
            fetch(piece).start()
        query_sums = jnp.zeros((rows, columns), jnp.float32)
        for piece in range(width // depth):
            fetch(piece).wait()
            start = piece * depth
            query_sums += jnp.dot(
                state(start, depth), weights[start : start + depth], preferred_element_type=jnp.float32
            )
        stacked = jnp.concatenate(
            [query_sums[:, h * head_size : (h + 1) * head_size] for h in range(heads)], axis=0
        )
        queries = unit(stacked).astype(jnp.bfloat16)
        image_rows = rows_ref[batch if rows_ref.shape[0] == SECTIONS else batch >> 1]
        scores = lax.dot_general(
            queries,
            image_rows[:, :head_size],
            (((1,), (1,)), ((), ())),
            preferred_element_type=jnp.float32,
        ) / math.sqrt(head_size)
        exponent = jnp.exp(scores)
        probs = (exponent / jnp.sum(exponent, axis=-1, keepdims=True)).astype(jnp.bfloat16)
        attended = jnp.dot(probs, image_rows[:, head_size:], preferred_element_type=jnp.float32)
        attended = attended.astype(jnp.bfloat16)
        attended = jnp.concatenate(
            [attended[h * rows : (h + 1) * rows] for h in range(heads)], axis=1
        )
        positions = lax.broadcasted_iota(jnp.int32, (rows, 1), 0)
        seen = (positions >= first_seen_ref[batch]).astype(jnp.float32)
        for start in range(0, width, columns):
            if start % depth == 0:
                fetch((width + start) // depth).wait()
            block = weights[width + start : width + start + columns]
            update = jnp.dot(attended, block, preferred_element_type=jnp.float32)
            result = state(start, columns).astype(jnp.float32) + seen * update
            out_ref[:, start : start + columns] = result.astype(jnp.bfloat16)

    for index in range(arrivals):

        @pl.when(jnp.logical_and(jnp.logical_not(active), chosen == index))
        def _(index=index):
            out_ref[...] = states[index][...]


def stack_kernel(w_query_ref, w_out_ref, out_ref, held, in_sems, out_sems):
    width, columns = w_query_ref.shape
    pieces = in_sems.shape[0]
    arriving, leaving = [], []
    for piece in range(pieces):
        rows = pl.ds(piece * columns, columns)
        below = piece * columns - width
        if below < 0:
            source = w_query_ref.at[rows, :]
        else:
            source = w_out_ref.at[:, pl.ds(below, columns)]
        arriving.append(pltpu.make_async_copy(source, held.at[rows, :], in_sems.at[piece]))
        leaving.append(pltpu.make_async_copy(held.at[rows, :], out_ref.at[rows, :], out_sems.at[piece]))
    for copy in arriving:
        copy.start()
    for piece in range(pieces):
        arriving[piece].wait()
        leaving[piece].start()
    for copy in leaving:
        copy.wait()


def stacked_weights(w_query, w_out):
    width, columns = w_query.shape
    return pl.pallas_call(
        stack_kernel,
        out_shape=jax.ShapeDtypeStruct((2 * width, columns), w_query.dtype),
        in_specs=[pl.BlockSpec(memory_space=pl.ANY)] * 2,
        out_specs=pl.BlockSpec(memory_space=pl.ANY),
        scratch_shapes=[
            pltpu.VMEM((2 * width, columns), w_query.dtype),
            pltpu.SemaphoreType.DMA((2 * width // columns,)),
            pltpu.SemaphoreType.DMA((2 * width // columns,)),
        ],
        compiler_params=pltpu.CompilerParams(vmem_limit_bytes=60 * 2**20),
        cost_estimate=pl.CostEstimate(
            flops=0, bytes_accessed=8 * width * columns, transcendentals=0
        ),
    )(w_query, w_out)


def slot_own(section):
    return section >= 0, section, 0


def slot_second(section):
    return (section & 1) == 0, section, 0


def slot_ahead(section):
    return section == 3, jnp.int32(1), 0


def slot_third(section):
    odd = jnp.where(section == 3, 1, 0)
    return section >= 2, odd, odd


def slot_fourth(section):
    kept = jnp.where(section == 1, 1, jnp.where(section == 3, 2, 0))
    return section == 2, jnp.int32(0), kept


def layer(slot, section, first_seen, states, rows_by_batch, weights, choosing=1):
    rows, width = states[0].shape
    columns = weights.shape[1]
    smem = pl.BlockSpec(memory_space=pltpu.SMEM)
    vmem = pl.BlockSpec(memory_space=pltpu.VMEM)
    return pl.pallas_call(
        functools.partial(layer_kernel, slot, len(states), choosing),
        out_shape=jax.ShapeDtypeStruct((rows, width), states[0].dtype),
        in_specs=[smem] * 2
        + [vmem] * (len(states) + 1)
        + [pl.BlockSpec(memory_space=pl.ANY)],
        out_specs=vmem,
        scratch_shapes=[
            pltpu.VMEM(weights.shape, weights.dtype),
            pltpu.SemaphoreType.DMA((2 * max(1, width // (2 * columns)),)),
        ],
        compiler_params=pltpu.CompilerParams(vmem_limit_bytes=VMEM_LIMIT),
        cost_estimate=pl.CostEstimate(
            flops=4 * rows * width * columns,
            bytes_accessed=4 * width * columns,
            transcendentals=rows * columns,
        ),
    )(section, first_seen, *states, rows_by_batch, weights)


def exchanged(block, axis, distance):
    devices = range(lax.axis_size(axis))
    return lax.ppermute(block, axis, [(i, i ^ distance) for i in devices])


def doubled(known, axis, distance, where):
    other = exchanged(known, axis, distance)
    upper = (lax.axis_index(axis) & distance) != 0
    first = jnp.where(upper, other, known)
    second = jnp.where(upper, known, other)
    return jnp.stack([first, second], axis=where)


def joined(known, axis, distance):
    known = doubled(known, axis, distance, 1)
    return known if axis == "yh" else known.reshape((-1,) + known.shape[2:])


def in_order(own, blocks):
    low, high = (own & 1) != 0, (own & 2) != 0
    near = [jnp.where(low, blocks[1], blocks[0]), jnp.where(low, blocks[0], blocks[1])]
    far = [jnp.where(low, blocks[3], blocks[2]), jnp.where(low, blocks[2], blocks[3])]
    first = [jnp.where(high, f, n) for n, f in zip(near, far)]
    second = [jnp.where(high, n, f) for n, f in zip(near, far)]
    return jnp.stack(first + second)


def joined_four(known, distance):
    blocks = {0: known}
    for step in (2, 1, 3):
        blocks[step] = exchanged(known, "z", step * distance)
    own = (lax.axis_index("z") // distance) & 3
    ordered = in_order(own, blocks)
    return ordered.reshape((-1,) + known.shape[1:])


def column_slices(image_states):
    width = image_states.shape[2]
    parts = lax.axis_size("x")
    own = lax.axis_index("x")
    depth = width // parts

    def columns(plane):
        return lax.dynamic_slice_in_dim(image_states, plane * depth, depth, 2)

    blocks = [columns(own)]
    for distance in range(1, parts):
        blocks.append(exchanged(columns(own ^ distance), "x", distance))
    return blocks


def local(
    text_states,
    image_states,
    image_start,
    w_query,
    w_key,
    w_value,
    w_out,
    query_gain,
    key_gain,
    cross_gate,
):
    sections = lax.axis_size("pipe")
    section_index = lax.axis_index("pipe")
    head_size = w_key.shape[2]
    known = jnp.concatenate([w_key[0], w_value[0]], axis=1)[None]
    known = joined(known, "yh", 1)
    known, image_states = lax.optimization_barrier((known, image_states))
    distance = lax.axis_size("z") // 4
    known = joined_four(known, distance)
    slices = column_slices(image_states)
    known, slices = lax.optimization_barrier((known, slices))
    ordered = in_order(lax.axis_index("x"), slices)
    halves = doubled(ordered, "pipe", 2, 0)
    distance //= 2
    known = joined(known, "z", distance)
    known, halves, w_query, w_out = lax.optimization_barrier((known, halves, w_query, w_out))
    pictures = doubled(halves, "pipe", 1, 1)
    own_weights = stacked_weights(w_query[0], w_out[0])
    distance //= 2
    known = joined(known, "z", distance)
    known, pictures = lax.optimization_barrier((known, pictures))
    pictures = pictures.reshape((-1,) + ordered.shape)
    while distance > 1:
        distance //= 2
        known = joined(known, "z", distance)
    known, own_weights = lax.optimization_barrier((known, own_weights))
    near_weights = exchanged(own_weights, "pipe", 1)
    weights = known.reshape(-1, known.shape[-1])
    parts, depth = lax.axis_size("x"), weights.shape[0]
    sums = jnp.dot(pictures.reshape(-1, depth), weights, preferred_element_type=jnp.float32)
    sums = sums.reshape(pictures.shape[:-1] + (2 * head_size,))
    own = lax.axis_index("x")
    total = lax.dynamic_index_in_dim(sums, own, 1, keepdims=False)
    rounded = sums.astype(jnp.bfloat16)
    for distance in range(1, parts):
        block = lax.dynamic_index_in_dim(rounded, own ^ distance, 1, keepdims=False)
        total = total + exchanged(block, "x", distance).astype(jnp.float32)
    total = jnp.swapaxes(total, 0, 1)
    total = total.reshape(total.shape[0], -1, 2 * head_size)
    key_scale = key_gain * query_gain
    key_rows = (unit(total[..., :head_size]) * key_scale[0]).astype(jnp.bfloat16)
    value_rows = (total[..., head_size:] * jnp.tanh(cross_gate[0])).astype(jnp.bfloat16)
    own_rows = jnp.concatenate([key_rows, value_rows], axis=-1)
    parity = section_index & 1
    by_parity = own_rows.reshape((sections // 2, 2) + own_rows.shape[1:])
    near_rows = exchanged(
        lax.dynamic_index_in_dim(by_parity, 1 - parity, 1, keepdims=False), "pipe", 1
    )
    section = section_index[None]
    first_seen = image_start[:, 0]
    run = functools.partial(layer, section=section, first_seen=first_seen)
    own = dict(rows_by_batch=own_rows, weights=own_weights)
    near = dict(rows_by_batch=near_rows, weights=near_weights)
    first = run(slot_own, states=(text_states[0],), **own)
    from_odd = lax.ppermute(first, "pipe", [(1, 3)])
    second = run(slot_second, states=(first,), **near)
    from_even = lax.ppermute(second, "pipe", [(0, 2)])
    ahead = run(slot_ahead, states=(from_odd,), **near)
    third = run(slot_third, states=(from_even, ahead), choosing=2, **own)
    home_odd = lax.ppermute(third, "pipe", [(3, 1)])
    fourth = run(slot_fourth, states=(third, home_odd, second), **near)
    home_even = lax.ppermute(fourth, "pipe", [(2, 0)])
    kept_state = jnp.where(section_index == 2, second, fourth)
    return jnp.where(section_index == 0, home_even, kept_state)[None]


def solution(mesh):
    sections = mesh.shape["pipe"]
    planes, far = 4, 2
    groups = mesh.shape["dp"] // (planes * far)
    mesh = Mesh(mesh.devices.reshape(planes, groups, far, sections), ("x", "z", "yh", "pipe"))
    replicas = ("x", "z", "yh")
    placed = (
        P("pipe", replicas, None),
        P(None, replicas + ("pipe",), None),
        P(None, replicas),
        P("pipe", None, None),
        P("pipe", replicas, None),
        P("pipe", replicas, None),
        P("pipe", None, None),
        P("pipe", None),
        P("pipe", None),
        P("pipe"),
    )
    return jax.shard_map(
        local, mesh=mesh, in_specs=placed, out_specs=P("pipe", replicas, None), check_vma=False
    )
```

```python
import functools
import math

import jax
import jax.numpy as jnp
from jax import lax
from jax.experimental import pallas as pl
from jax.experimental.pallas import tpu as pltpu
from jax.sharding import Mesh
from jax.sharding import PartitionSpec as P

epsilon = 1e-06
VMEM_LIMIT = 24 * 2**20
SECTIONS = 4


def unit(projected):
    mean_square = jnp.mean(projected * projected, axis=-1, keepdims=True)
    return projected * lax.rsqrt(mean_square + epsilon)


def layer_kernel(slot, arrivals, choosing, section_ref, first_seen_ref, *refs):
    states = refs[:arrivals]
    rows_ref, weights, out_ref = refs[arrivals:]
    rows, width = out_ref.shape
    columns = weights.shape[1]
    head_size = rows_ref.shape[2] // 2
    heads = columns // head_size
    depth = min(width, 2 * columns)
    active, batch, chosen = slot(section_ref[0])

    def state(start, size):
        held = states[0][:, start : start + size]
        for index in range(1, choosing):
            held = jnp.where(chosen == index, states[index][:, start : start + size], held)
        return held

    @pl.when(active)
    def _():
        query_sums = jnp.zeros((rows, columns), jnp.float32)
        for piece in range(width // depth):
            start = piece * depth
            query_sums += jnp.dot(
                state(start, depth), weights[start : start + depth], preferred_element_type=jnp.float32
            )
        stacked = jnp.concatenate(
            [query_sums[:, h * head_size : (h + 1) * head_size] for h in range(heads)], axis=0
        )
        queries = unit(stacked).astype(jnp.bfloat16)
        image_rows = rows_ref[batch if rows_ref.shape[0] == SECTIONS else batch >> 1]
        scores = lax.dot_general(
            queries,
            image_rows[:, :head_size],
            (((1,), (1,)), ((), ())),
            preferred_element_type=jnp.float32,
        ) / math.sqrt(head_size)
        exponent = jnp.exp(scores)
        probs = (exponent / jnp.sum(exponent, axis=-1, keepdims=True)).astype(jnp.bfloat16)
        attended = jnp.dot(probs, image_rows[:, head_size:], preferred_element_type=jnp.float32)
        attended = attended.astype(jnp.bfloat16)
        attended = jnp.concatenate(
            [attended[h * rows : (h + 1) * rows] for h in range(heads)], axis=1
        )
        positions = lax.broadcasted_iota(jnp.int32, (rows, 1), 0)
        seen = (positions >= first_seen_ref[batch]).astype(jnp.float32)
        for start in range(0, width, columns):
            block = weights[width + start : width + start + columns]
            update = jnp.dot(attended, block, preferred_element_type=jnp.float32)
            result = state(start, columns).astype(jnp.float32) + seen * update
            out_ref[:, start : start + columns] = result.astype(jnp.bfloat16)

    for index in range(arrivals):

        @pl.when(jnp.logical_and(jnp.logical_not(active), chosen == index))
        def _(index=index):
            out_ref[...] = states[index][...]


def stack_kernel(w_query_ref, w_out_ref, out_ref, sems):
    width, columns = w_query_ref.shape
    arriving = []
    for piece in range(sems.shape[0]):
        rows = pl.ds(piece * columns, columns)
        below = piece * columns - width
        if below < 0:
            source = w_query_ref.at[rows, :]
        else:
            source = w_out_ref.at[:, pl.ds(below, columns)]
        arriving.append(pltpu.make_async_copy(source, out_ref.at[rows, :], sems.at[piece]))
    for copy in arriving:
        copy.start()
    for copy in arriving:
        copy.wait()


def stacked_weights(w_query, w_out):
    width, columns = w_query.shape
    return pl.pallas_call(
        stack_kernel,
        out_shape=jax.ShapeDtypeStruct((2 * width, columns), w_query.dtype),
        in_specs=[pl.BlockSpec(memory_space=pl.ANY)] * 2,
        out_specs=pl.BlockSpec(memory_space=pltpu.VMEM),
        scratch_shapes=[pltpu.SemaphoreType.DMA((2 * width // columns,))],
        compiler_params=pltpu.CompilerParams(vmem_limit_bytes=VMEM_LIMIT),
        cost_estimate=pl.CostEstimate(
            flops=0, bytes_accessed=8 * width * columns, transcendentals=0
        ),
    )(w_query, w_out)


def slot_own(section):
    return section >= 0, section, 0


def slot_second(section):
    return (section & 1) == 0, section, 0


def slot_ahead(section):
    return section == 3, jnp.int32(1), 0


def slot_third(section):
    odd = jnp.where(section == 3, 1, 0)
    return section >= 2, odd, odd


def slot_fourth(section):
    kept = jnp.where(section == 1, 1, jnp.where(section == 3, 2, 0))
    return section == 2, jnp.int32(0), kept


def layer(slot, section, first_seen, states, rows_by_batch, weights, choosing=1):
    rows, width = states[0].shape
    columns = weights.shape[1]
    smem = pl.BlockSpec(memory_space=pltpu.SMEM)
    vmem = pl.BlockSpec(memory_space=pltpu.VMEM)
    return pl.pallas_call(
        functools.partial(layer_kernel, slot, len(states), choosing),
        out_shape=jax.ShapeDtypeStruct((rows, width), states[0].dtype),
        in_specs=[smem] * 2
        + [vmem] * (len(states) + 2),
        out_specs=vmem,
        compiler_params=pltpu.CompilerParams(vmem_limit_bytes=VMEM_LIMIT),
        cost_estimate=pl.CostEstimate(
            flops=4 * rows * width * columns,
            bytes_accessed=4 * width * columns,
            transcendentals=rows * columns,
        ),
    )(section, first_seen, *states, rows_by_batch, weights)


def exchanged(block, axis, distance):
    devices = range(lax.axis_size(axis))
    return lax.ppermute(block, axis, [(i, i ^ distance) for i in devices])


def doubled(known, axis, distance, where):
    other = exchanged(known, axis, distance)
    upper = (lax.axis_index(axis) & distance) != 0
    first = jnp.where(upper, other, known)
    second = jnp.where(upper, known, other)
    return jnp.stack([first, second], axis=where)


def joined(known, axis, distance):
    known = doubled(known, axis, distance, 1)
    return known if axis == "yh" else known.reshape((-1,) + known.shape[2:])


def in_order(own, blocks):
    low, high = (own & 1) != 0, (own & 2) != 0
    near = [jnp.where(low, blocks[1], blocks[0]), jnp.where(low, blocks[0], blocks[1])]
    far = [jnp.where(low, blocks[3], blocks[2]), jnp.where(low, blocks[2], blocks[3])]
    first = [jnp.where(high, f, n) for n, f in zip(near, far)]
    second = [jnp.where(high, n, f) for n, f in zip(near, far)]
    return jnp.stack(first + second)


def joined_four(known, distance):
    blocks = {0: known}
    for step in (2, 1, 3):
        blocks[step] = exchanged(known, "z", step * distance)
    own = (lax.axis_index("z") // distance) & 3
    ordered = in_order(own, blocks)
    return ordered.reshape((-1,) + known.shape[1:])


def column_slices(image_states):
    width = image_states.shape[2]
    parts = lax.axis_size("x")
    own = lax.axis_index("x")
    depth = width // parts

    def columns(plane):
        return lax.dynamic_slice_in_dim(image_states, plane * depth, depth, 2)

    blocks = [columns(own)]
    for distance in range(1, parts):
        blocks.append(exchanged(columns(own ^ distance), "x", distance))
    return blocks


def local(
    text_states,
    image_states,
    image_start,
    w_query,
    w_key,
    w_value,
    w_out,
    query_gain,
    key_gain,
    cross_gate,
):
    sections = lax.axis_size("pipe")
    section_index = lax.axis_index("pipe")
    head_size = w_key.shape[2]
    known = jnp.concatenate([w_key[0], w_value[0]], axis=1)[None]
    known = joined(known, "yh", 1)
    known, image_states = lax.optimization_barrier((known, image_states))
    distance = lax.axis_size("z") // 4
    known = joined_four(known, distance)
    slices = column_slices(image_states)
    known, slices = lax.optimization_barrier((known, slices))
    ordered = in_order(lax.axis_index("x"), slices)
    halves = doubled(ordered, "pipe", 2, 0)
    distance //= 2
    known = joined(known, "z", distance)
    known, halves, w_query, w_out = lax.optimization_barrier((known, halves, w_query, w_out))
    pictures = doubled(halves, "pipe", 1, 1)
    own_weights = stacked_weights(w_query[0], w_out[0])
    distance //= 2
    known = joined(known, "z", distance)
    known, pictures = lax.optimization_barrier((known, pictures))
    pictures = pictures.reshape((-1,) + ordered.shape)
    while distance > 1:
        distance //= 2
        known = joined(known, "z", distance)
    known, own_weights = lax.optimization_barrier((known, own_weights))
    near_weights = exchanged(own_weights, "pipe", 1)
    weights = known.reshape(-1, known.shape[-1])
    parts, depth = lax.axis_size("x"), weights.shape[0]
    sums = jnp.dot(pictures.reshape(-1, depth), weights, preferred_element_type=jnp.float32)
    sums = sums.reshape(pictures.shape[:-1] + (2 * head_size,))
    own = lax.axis_index("x")
    total = lax.dynamic_index_in_dim(sums, own, 1, keepdims=False)
    rounded = sums.astype(jnp.bfloat16)
    for distance in range(1, parts):
        block = lax.dynamic_index_in_dim(rounded, own ^ distance, 1, keepdims=False)
        total = total + exchanged(block, "x", distance).astype(jnp.float32)
    total = jnp.swapaxes(total, 0, 1)
    total = total.reshape(total.shape[0], -1, 2 * head_size)
    key_scale = key_gain * query_gain
    key_rows = (unit(total[..., :head_size]) * key_scale[0]).astype(jnp.bfloat16)
    value_rows = (total[..., head_size:] * jnp.tanh(cross_gate[0])).astype(jnp.bfloat16)
    own_rows = jnp.concatenate([key_rows, value_rows], axis=-1)
    parity = section_index & 1
    by_parity = own_rows.reshape((sections // 2, 2) + own_rows.shape[1:])
    near_rows = exchanged(
        lax.dynamic_index_in_dim(by_parity, 1 - parity, 1, keepdims=False), "pipe", 1
    )
    section = section_index[None]
    first_seen = image_start[:, 0]
    run = functools.partial(layer, section=section, first_seen=first_seen)
    own = dict(rows_by_batch=own_rows, weights=own_weights)
    near = dict(rows_by_batch=near_rows, weights=near_weights)
    first = run(slot_own, states=(text_states[0],), **own)
    from_odd = lax.ppermute(first, "pipe", [(1, 3)])
    second = run(slot_second, states=(first,), **near)
    from_even = lax.ppermute(second, "pipe", [(0, 2)])
    ahead = run(slot_ahead, states=(from_odd,), **near)
    third = run(slot_third, states=(from_even, ahead), choosing=2, **own)
    home_odd = lax.ppermute(third, "pipe", [(3, 1)])
    fourth = run(slot_fourth, states=(third, home_odd, second), **near)
    home_even = lax.ppermute(fourth, "pipe", [(2, 0)])
    kept_state = jnp.where(section_index == 2, second, fourth)
    return jnp.where(section_index == 0, home_even, kept_state)[None]


def solution(mesh):
    sections = mesh.shape["pipe"]
    planes, far = 4, 2
    groups = mesh.shape["dp"] // (planes * far)
    mesh = Mesh(mesh.devices.reshape(planes, groups, far, sections), ("x", "z", "yh", "pipe"))
    replicas = ("x", "z", "yh")
    placed = (
        P("pipe", replicas, None),
        P(None, replicas + ("pipe",), None),
        P(None, replicas),
        P("pipe", None, None),
        P("pipe", replicas, None),
        P("pipe", replicas, None),
        P("pipe", None, None),
        P("pipe", None),
        P("pipe", None),
        P("pipe"),
    )
    return jax.shard_map(
        local, mesh=mesh, in_specs=placed, out_specs=P("pipe", replicas, None), check_vma=False
    )
```

```python
import functools
import math

import jax
import jax.numpy as jnp
from jax import lax
from jax.experimental import pallas as pl
from jax.experimental.pallas import tpu as pltpu
from jax.sharding import Mesh
from jax.sharding import PartitionSpec as P

epsilon = 1e-06
VMEM_LIMIT = 48 * 2**20
SECTIONS = 4


def unit(projected):
    mean_square = jnp.mean(projected * projected, axis=-1, keepdims=True)
    return projected * lax.rsqrt(mean_square + epsilon)


def layer_kernel(slot, arrivals, choosing, given, section_ref, first_seen_ref, *refs):
    states = refs[:arrivals]
    rows_ref, weights_ref, *sums_ref, out_ref, weights, sems = refs[arrivals:]
    rows, width = out_ref.shape
    columns = weights.shape[1]
    head_size = rows_ref.shape[2] // 2
    heads = columns // head_size
    pieces = sems.shape[0]
    depth = weights.shape[0] // pieces
    active, batch, chosen = slot(section_ref[0])

    def fetch(piece):
        rows_of = pl.ds(piece * depth, depth)
        return pltpu.make_async_copy(weights_ref.at[rows_of, :], weights.at[rows_of, :], sems.at[piece])

    def state(start, size):
        held = states[0][:, start : start + size]
        for index in range(1, choosing):
            held = jnp.where(chosen == index, states[index][:, start : start + size], held)
        return held

    @pl.when(active)
    def _():
        for piece in range(width // depth if given else 0, pieces):
            fetch(piece).start()
        query_sums = sums_ref[0][...] if given else jnp.zeros((rows, columns), jnp.float32)
        for piece in range(0 if given else width // depth):
            fetch(piece).wait()
            start = piece * depth
            query_sums += jnp.dot(
                state(start, depth), weights[start : start + depth], preferred_element_type=jnp.float32
            )
        stacked = jnp.concatenate(
            [query_sums[:, h * head_size : (h + 1) * head_size] for h in range(heads)], axis=0
        )
        queries = unit(stacked).astype(jnp.bfloat16)
        image_rows = rows_ref[batch if rows_ref.shape[0] == SECTIONS else batch >> 1]
        scores = lax.dot_general(
            queries,
            image_rows[:, :head_size],
            (((1,), (1,)), ((), ())),
            preferred_element_type=jnp.float32,
        ) / math.sqrt(head_size)
        exponent = jnp.exp(scores)
        probs = (exponent / jnp.sum(exponent, axis=-1, keepdims=True)).astype(jnp.bfloat16)
        attended = jnp.dot(probs, image_rows[:, head_size:], preferred_element_type=jnp.float32)
        attended = attended.astype(jnp.bfloat16)
        attended = jnp.concatenate(
            [attended[h * rows : (h + 1) * rows] for h in range(heads)], axis=1
        )
        positions = lax.broadcasted_iota(jnp.int32, (rows, 1), 0)
        seen = (positions >= first_seen_ref[batch]).astype(jnp.float32)
        for start in range(0, width, columns):
            if start % depth == 0:
                fetch((width + start) // depth).wait()
            block = weights[width + start : width + start + columns]
            update = jnp.dot(attended, block, preferred_element_type=jnp.float32)
            result = state(start, columns).astype(jnp.float32) + seen * update
            out_ref[:, start : start + columns] = result.astype(jnp.bfloat16)

    for index in range(arrivals):

        @pl.when(jnp.logical_and(jnp.logical_not(active), chosen == index))
        def _(index=index):
            out_ref[...] = states[index][...]


def stack_kernel(w_query_ref, w_out_ref, out_ref, held, in_sems, out_sems):
    width, columns = w_query_ref.shape
    pieces = in_sems.shape[0]
    arriving, leaving = [], []
    for piece in range(pieces):
        rows = pl.ds(piece * columns, columns)
        below = piece * columns - width
        if below < 0:
            source = w_query_ref.at[rows, :]
        else:
            source = w_out_ref.at[:, pl.ds(below, columns)]
        arriving.append(pltpu.make_async_copy(source, held.at[rows, :], in_sems.at[piece]))
        leaving.append(pltpu.make_async_copy(held.at[rows, :], out_ref.at[rows, :], out_sems.at[piece]))
    for copy in arriving:
        copy.start()
    for piece in range(pieces):
        arriving[piece].wait()
        leaving[piece].start()
    for copy in leaving:
        copy.wait()


def stacked_weights(w_query, w_out):
    width, columns = w_query.shape
    return pl.pallas_call(
        stack_kernel,
        out_shape=jax.ShapeDtypeStruct((2 * width, columns), w_query.dtype),
        in_specs=[pl.BlockSpec(memory_space=pl.ANY)] * 2,
        out_specs=pl.BlockSpec(memory_space=pl.ANY),
        scratch_shapes=[
            pltpu.VMEM((2 * width, columns), w_query.dtype),
            pltpu.SemaphoreType.DMA((2 * width // columns,)),
            pltpu.SemaphoreType.DMA((2 * width // columns,)),
        ],
        compiler_params=pltpu.CompilerParams(vmem_limit_bytes=60 * 2**20),
        cost_estimate=pl.CostEstimate(
            flops=0, bytes_accessed=8 * width * columns, transcendentals=0
        ),
    )(w_query, w_out)


def slot_own(section):
    return section >= 0, section, 0


def slot_second(section):
    return (section & 1) == 0, section, 0


def slot_ahead(section):
    return section == 3, jnp.int32(1), 0


def slot_third(section):
    odd = jnp.where(section == 3, 1, 0)
    return section >= 2, odd, odd


def slot_fourth(section):
    kept = jnp.where(section == 1, 1, jnp.where(section == 3, 2, 0))
    return section == 2, jnp.int32(0), kept


def layer(slot, section, first_seen, states, rows_by_batch, weights, choosing=1, sums=()):
    rows, width = states[0].shape
    columns = weights.shape[1]
    smem = pl.BlockSpec(memory_space=pltpu.SMEM)
    vmem = pl.BlockSpec(memory_space=pltpu.VMEM)
    return pl.pallas_call(
        functools.partial(layer_kernel, slot, len(states), choosing, len(sums) == 1),
        out_shape=jax.ShapeDtypeStruct((rows, width), states[0].dtype),
        in_specs=[smem] * 2
        + [vmem] * (len(states) + 1)
        + [pl.BlockSpec(memory_space=pl.ANY)]
        + [vmem] * len(sums),
        out_specs=vmem,
        scratch_shapes=[
            pltpu.VMEM(weights.shape, weights.dtype),
            pltpu.SemaphoreType.DMA((2 * max(1, width // (2 * columns)),)),
        ],
        compiler_params=pltpu.CompilerParams(vmem_limit_bytes=VMEM_LIMIT),
        cost_estimate=pl.CostEstimate(
            flops=4 * rows * width * columns,
            bytes_accessed=4 * width * columns,
            transcendentals=rows * columns,
        ),
    )(section, first_seen, *states, rows_by_batch, weights, *sums)


def exchanged(block, axis, distance):
    devices = range(lax.axis_size(axis))
    return lax.ppermute(block, axis, [(i, i ^ distance) for i in devices])


def doubled(known, axis, distance, where):
    other = exchanged(known, axis, distance)
    upper = (lax.axis_index(axis) & distance) != 0
    first = jnp.where(upper, other, known)
    second = jnp.where(upper, known, other)
    return jnp.stack([first, second], axis=where)


def joined(known, axis, distance):
    known = doubled(known, axis, distance, 1)
    return known if axis == "yh" else known.reshape((-1,) + known.shape[2:])


def in_order(own, blocks):
    low, high = (own & 1) != 0, (own & 2) != 0
    near = [jnp.where(low, blocks[1], blocks[0]), jnp.where(low, blocks[0], blocks[1])]
    far = [jnp.where(low, blocks[3], blocks[2]), jnp.where(low, blocks[2], blocks[3])]
    first = [jnp.where(high, f, n) for n, f in zip(near, far)]
    second = [jnp.where(high, n, f) for n, f in zip(near, far)]
    return jnp.stack(first + second)


def joined_four(known, distance):
    blocks = {0: known}
    for step in (2, 1, 3):
        blocks[step] = exchanged(known, "z", step * distance)
    own = (lax.axis_index("z") // distance) & 3
    ordered = in_order(own, blocks)
    return ordered.reshape((-1,) + known.shape[1:])


def column_slices(image_states):
    width = image_states.shape[2]
    parts = lax.axis_size("x")
    own = lax.axis_index("x")
    depth = width // parts

    def columns(plane):
        return lax.dynamic_slice_in_dim(image_states, plane * depth, depth, 2)

    blocks = [columns(own)]
    for distance in range(1, parts):
        blocks.append(exchanged(columns(own ^ distance), "x", distance))
    return blocks


def local(
    text_states,
    image_states,
    image_start,
    w_query,
    w_key,
    w_value,
    w_out,
    query_gain,
    key_gain,
    cross_gate,
):
    sections = lax.axis_size("pipe")
    section_index = lax.axis_index("pipe")
    head_size = w_key.shape[2]
    known = jnp.concatenate([w_key[0], w_value[0]], axis=1)[None]
    known = joined(known, "yh", 1)
    known, image_states = lax.optimization_barrier((known, image_states))
    distance = lax.axis_size("z") // 4
    known = joined_four(known, distance)
    slices = column_slices(image_states)
    known, slices = lax.optimization_barrier((known, slices))
    ordered = in_order(lax.axis_index("x"), slices)
    halves = doubled(ordered, "pipe", 2, 0)
    distance //= 2
    known = joined(known, "z", distance)
    known, halves, w_query, w_out = lax.optimization_barrier((known, halves, w_query, w_out))
    pictures = doubled(halves, "pipe", 1, 1)
    query_sums = jnp.dot(text_states[0], w_query[0], preferred_element_type=jnp.float32)
    own_weights = stacked_weights(w_query[0], w_out[0])
    distance //= 2
    known = joined(known, "z", distance)
    known, pictures = lax.optimization_barrier((known, pictures))
    pictures = pictures.reshape((-1,) + ordered.shape)
    while distance > 1:
        distance //= 2
        known = joined(known, "z", distance)
    known, own_weights = lax.optimization_barrier((known, own_weights))
    near_weights = exchanged(own_weights, "pipe", 1)
    weights = known.reshape(-1, known.shape[-1])
    parts, depth = lax.axis_size("x"), weights.shape[0]
    sums = jnp.dot(pictures.reshape(-1, depth), weights, preferred_element_type=jnp.float32)
    sums = sums.reshape(pictures.shape[:-1] + (2 * head_size,))
    own = lax.axis_index("x")
    total = lax.dynamic_index_in_dim(sums, own, 1, keepdims=False)
    rounded = sums.astype(jnp.bfloat16)
    for distance in range(1, parts):
        block = lax.dynamic_index_in_dim(rounded, own ^ distance, 1, keepdims=False)
        total = total + exchanged(block, "x", distance).astype(jnp.float32)
    total, query_sums = lax.optimization_barrier((total, query_sums))
    total = jnp.swapaxes(total, 0, 1)
    total = total.reshape(total.shape[0], -1, 2 * head_size)
    key_scale = key_gain * query_gain
    key_rows = (unit(total[..., :head_size]) * key_scale[0]).astype(jnp.bfloat16)
    value_rows = (total[..., head_size:] * jnp.tanh(cross_gate[0])).astype(jnp.bfloat16)
    own_rows = jnp.concatenate([key_rows, value_rows], axis=-1)
    parity = section_index & 1
    by_parity = own_rows.reshape((sections // 2, 2) + own_rows.shape[1:])
    near_rows = exchanged(
        lax.dynamic_index_in_dim(by_parity, 1 - parity, 1, keepdims=False), "pipe", 1
    )
    section = section_index[None]
    first_seen = image_start[:, 0]
    run = functools.partial(layer, section=section, first_seen=first_seen)
    own = dict(rows_by_batch=own_rows, weights=own_weights)
    near = dict(rows_by_batch=near_rows, weights=near_weights)
    first = run(slot_own, states=(text_states[0],), sums=(query_sums,), **own)
    from_odd = lax.ppermute(first, "pipe", [(1, 3)])
    second = run(slot_second, states=(first,), **near)
    from_even = lax.ppermute(second, "pipe", [(0, 2)])
    ahead = run(slot_ahead, states=(from_odd,), **near)
    third = run(slot_third, states=(from_even, ahead), choosing=2, **own)
    home_odd = lax.ppermute(third, "pipe", [(3, 1)])
    fourth = run(slot_fourth, states=(third, home_odd, second), **near)
    home_even = lax.ppermute(fourth, "pipe", [(2, 0)])
    kept_state = jnp.where(section_index == 2, second, fourth)
    return jnp.where(section_index == 0, home_even, kept_state)[None]


def solution(mesh):
    sections = mesh.shape["pipe"]
    planes, far = 4, 2
    groups = mesh.shape["dp"] // (planes * far)
    mesh = Mesh(mesh.devices.reshape(planes, groups, far, sections), ("x", "z", "yh", "pipe"))
    replicas = ("x", "z", "yh")
    placed = (
        P("pipe", replicas, None),
        P(None, replicas + ("pipe",), None),
        P(None, replicas),
        P("pipe", None, None),
        P("pipe", replicas, None),
        P("pipe", replicas, None),
        P("pipe", None, None),
        P("pipe", None),
        P("pipe", None),
        P("pipe"),
    )
    return jax.shard_map(
        local, mesh=mesh, in_specs=placed, out_specs=P("pipe", replicas, None), check_vma=False
    )
```

```python
import functools
import math

import jax
import jax.numpy as jnp
from jax import lax
from jax.experimental import pallas as pl
from jax.experimental.pallas import tpu as pltpu
from jax.sharding import Mesh
from jax.sharding import PartitionSpec as P

epsilon = 1e-06
VMEM_LIMIT = 48 * 2**20
SECTIONS = 4


def unit(projected):
    mean_square = jnp.mean(projected * projected, axis=-1, keepdims=True)
    return projected * lax.rsqrt(mean_square + epsilon)


def layer_kernel(slot, arrivals, choosing, given, section_ref, first_seen_ref, *refs):
    states = refs[:arrivals]
    rows_ref, weights_ref, *sums_ref, out_ref, weights, sems = refs[arrivals:]
    rows, width = out_ref.shape
    columns = weights.shape[1]
    head_size = rows_ref.shape[2] // 2
    heads = columns // head_size
    pieces = sems.shape[0]
    depth = weights.shape[0] // pieces
    active, batch, chosen = slot(section_ref[0])

    def fetch(piece):
        rows_of = pl.ds(piece * depth, depth)
        return pltpu.make_async_copy(weights_ref.at[rows_of, :], weights.at[rows_of, :], sems.at[piece])

    def state(start, size):
        held = states[0][:, start : start + size]
        for index in range(1, choosing):
            held = jnp.where(chosen == index, states[index][:, start : start + size], held)
        return held

    @pl.when(active)
    def _():
        for piece in range(width // depth if given else 0, pieces):
            fetch(piece).start()
        query_sums = sums_ref[0][...] if given else jnp.zeros((rows, columns), jnp.float32)
        for piece in range(0 if given else width // depth):
            fetch(piece).wait()
            start = piece * depth
            query_sums += jnp.dot(
                state(start, depth), weights[start : start + depth], preferred_element_type=jnp.float32
            )
        stacked = jnp.concatenate(
            [query_sums[:, h * head_size : (h + 1) * head_size] for h in range(heads)], axis=0
        )
        queries = unit(stacked).astype(jnp.bfloat16)
        image_rows = rows_ref[batch if rows_ref.shape[0] == SECTIONS else batch >> 1]
        scores = lax.dot_general(
            queries,
            image_rows[:, :head_size],
            (((1,), (1,)), ((), ())),
            preferred_element_type=jnp.float32,
        ) / math.sqrt(head_size)
        exponent = jnp.exp(scores)
        probs = (exponent / jnp.sum(exponent, axis=-1, keepdims=True)).astype(jnp.bfloat16)
        attended = jnp.dot(probs, image_rows[:, head_size:], preferred_element_type=jnp.float32)
        attended = attended.astype(jnp.bfloat16)
        attended = jnp.concatenate(
            [attended[h * rows : (h + 1) * rows] for h in range(heads)], axis=1
        )
        positions = lax.broadcasted_iota(jnp.int32, (rows, 1), 0)
        seen = (positions >= first_seen_ref[batch]).astype(jnp.float32)
        for start in range(0, width, columns):
            if start % depth == 0:
                fetch((width + start) // depth).wait()
            block = weights[width + start : width + start + columns]
            update = jnp.dot(attended, block, preferred_element_type=jnp.float32)
            result = state(start, columns).astype(jnp.float32) + seen * update
            out_ref[:, start : start + columns] = result.astype(jnp.bfloat16)

    for index in range(arrivals):

        @pl.when(jnp.logical_and(jnp.logical_not(active), chosen == index))
        def _(index=index):
            out_ref[...] = states[index][...]


def stack_kernel(w_query_ref, w_out_ref, out_ref, held, in_sems, out_sems):
    width, columns = w_query_ref.shape
    pieces = in_sems.shape[0]
    arriving, leaving = [], []
    for piece in range(pieces):
        rows = pl.ds(piece * columns, columns)
        below = piece * columns - width
        if below < 0:
            source = w_query_ref.at[rows, :]
        else:
            source = w_out_ref.at[:, pl.ds(below, columns)]
        arriving.append(pltpu.make_async_copy(source, held.at[rows, :], in_sems.at[piece]))
        leaving.append(pltpu.make_async_copy(held.at[rows, :], out_ref.at[rows, :], out_sems.at[piece]))
    for copy in arriving:
        copy.start()
    for piece in range(pieces):
        arriving[piece].wait()
        leaving[piece].start()
    for copy in leaving:
        copy.wait()


def stacked_weights(w_query, w_out):
    width, columns = w_query.shape
    return pl.pallas_call(
        stack_kernel,
        out_shape=jax.ShapeDtypeStruct((2 * width, columns), w_query.dtype),
        in_specs=[pl.BlockSpec(memory_space=pl.ANY)] * 2,
        out_specs=pl.BlockSpec(memory_space=pl.ANY),
        scratch_shapes=[
            pltpu.VMEM((2 * width, columns), w_query.dtype),
            pltpu.SemaphoreType.DMA((2 * width // columns,)),
            pltpu.SemaphoreType.DMA((2 * width // columns,)),
        ],
        compiler_params=pltpu.CompilerParams(vmem_limit_bytes=60 * 2**20),
        cost_estimate=pl.CostEstimate(
            flops=0, bytes_accessed=8 * width * columns, transcendentals=0
        ),
    )(w_query, w_out)


def slot_own(section):
    return section >= 0, section, 0


def slot_second(section):
    return (section & 1) == 0, section, 0


def slot_ahead(section):
    return section == 3, jnp.int32(1), 0


def slot_third(section):
    odd = jnp.where(section == 3, 1, 0)
    return section >= 2, odd, odd


def slot_fourth(section):
    kept = jnp.where(section == 1, 1, jnp.where(section == 3, 2, 0))
    return section == 2, jnp.int32(0), kept


def layer(slot, section, first_seen, states, rows_by_batch, weights, choosing=1, sums=()):
    rows, width = states[0].shape
    columns = weights.shape[1]
    smem = pl.BlockSpec(memory_space=pltpu.SMEM)
    vmem = pl.BlockSpec(memory_space=pltpu.VMEM)
    return pl.pallas_call(
        functools.partial(layer_kernel, slot, len(states), choosing, len(sums) == 1),
        out_shape=jax.ShapeDtypeStruct((rows, width), states[0].dtype),
        in_specs=[smem] * 2
        + [vmem] * (len(states) + 1)
        + [pl.BlockSpec(memory_space=pl.ANY)]
        + [vmem] * len(sums),
        out_specs=vmem,
        scratch_shapes=[
            pltpu.VMEM(weights.shape, weights.dtype),
            pltpu.SemaphoreType.DMA((2 * max(1, width // (2 * columns)),)),
        ],
        compiler_params=pltpu.CompilerParams(vmem_limit_bytes=VMEM_LIMIT),
        cost_estimate=pl.CostEstimate(
            flops=4 * rows * width * columns,
            bytes_accessed=4 * width * columns,
            transcendentals=rows * columns,
        ),
    )(section, first_seen, *states, rows_by_batch, weights, *sums)


def exchanged(block, axis, distance):
    devices = range(lax.axis_size(axis))
    return lax.ppermute(block, axis, [(i, i ^ distance) for i in devices])


def doubled(known, axis, distance, where):
    other = exchanged(known, axis, distance)
    upper = (lax.axis_index(axis) & distance) != 0
    first = jnp.where(upper, other, known)
    second = jnp.where(upper, known, other)
    return jnp.stack([first, second], axis=where)


def joined(known, axis, distance):
    known = doubled(known, axis, distance, 1)
    return known if axis == "yh" else known.reshape((-1,) + known.shape[2:])


def in_order(own, blocks):
    low, high = (own & 1) != 0, (own & 2) != 0
    near = [jnp.where(low, blocks[1], blocks[0]), jnp.where(low, blocks[0], blocks[1])]
    far = [jnp.where(low, blocks[3], blocks[2]), jnp.where(low, blocks[2], blocks[3])]
    first = [jnp.where(high, f, n) for n, f in zip(near, far)]
    second = [jnp.where(high, n, f) for n, f in zip(near, far)]
    return jnp.stack(first + second)


def joined_four(known, distance):
    blocks = {0: known}
    for step in (2, 1, 3):
        blocks[step] = exchanged(known, "z", step * distance)
    own = (lax.axis_index("z") // distance) & 3
    ordered = in_order(own, blocks)
    return ordered.reshape((-1,) + known.shape[1:])


def column_slices(image_states):
    width = image_states.shape[2]
    parts = lax.axis_size("x")
    own = lax.axis_index("x")
    depth = width // parts

    def columns(plane):
        return lax.dynamic_slice_in_dim(image_states, plane * depth, depth, 2)

    blocks = [columns(own)]
    for distance in range(1, parts):
        blocks.append(exchanged(columns(own ^ distance), "x", distance))
    return blocks


def local(
    text_states,
    image_states,
    image_start,
    w_query,
    w_key,
    w_value,
    w_out,
    query_gain,
    key_gain,
    cross_gate,
):
    sections = lax.axis_size("pipe")
    section_index = lax.axis_index("pipe")
    head_size = w_key.shape[2]
    known = jnp.concatenate([w_key[0], w_value[0]], axis=1)[None]
    known = joined(known, "yh", 1)
    known, image_states = lax.optimization_barrier((known, image_states))
    distance = lax.axis_size("z") // 4
    known = joined_four(known, distance)
    slices = column_slices(image_states)
    known, slices = lax.optimization_barrier((known, slices))
    ordered = in_order(lax.axis_index("x"), slices)
    distance //= 2
    known = joined(known, "z", distance)
    known, ordered, w_query, w_out = lax.optimization_barrier((known, ordered, w_query, w_out))
    halves = doubled(ordered, "pipe", 2, 0)
    query_sums = jnp.dot(text_states[0], w_query[0], preferred_element_type=jnp.float32)
    own_weights = stacked_weights(w_query[0], w_out[0])
    distance //= 2
    known = joined(known, "z", distance)
    known, halves = lax.optimization_barrier((known, halves))
    pictures = doubled(halves, "pipe", 1, 1).reshape((-1,) + ordered.shape)
    while distance > 1:
        distance //= 2
        known = joined(known, "z", distance)
    known, own_weights = lax.optimization_barrier((known, own_weights))
    near_weights = exchanged(own_weights, "pipe", 1)
    weights = known.reshape(-1, known.shape[-1])
    parts, depth = lax.axis_size("x"), weights.shape[0]
    sums = jnp.dot(pictures.reshape(-1, depth), weights, preferred_element_type=jnp.float32)
    sums = sums.reshape(pictures.shape[:-1] + (2 * head_size,))
    own = lax.axis_index("x")
    total = lax.dynamic_index_in_dim(sums, own, 1, keepdims=False)
    rounded = sums.astype(jnp.bfloat16)
    for distance in range(1, parts):
        block = lax.dynamic_index_in_dim(rounded, own ^ distance, 1, keepdims=False)
        total = total + exchanged(block, "x", distance).astype(jnp.float32)
    total, query_sums = lax.optimization_barrier((total, query_sums))
    total = jnp.swapaxes(total, 0, 1)
    total = total.reshape(total.shape[0], -1, 2 * head_size)
    key_scale = key_gain * query_gain
    key_rows = (unit(total[..., :head_size]) * key_scale[0]).astype(jnp.bfloat16)
    value_rows = (total[..., head_size:] * jnp.tanh(cross_gate[0])).astype(jnp.bfloat16)
    own_rows = jnp.concatenate([key_rows, value_rows], axis=-1)
    parity = section_index & 1
    by_parity = own_rows.reshape((sections // 2, 2) + own_rows.shape[1:])
    near_rows = exchanged(
        lax.dynamic_index_in_dim(by_parity, 1 - parity, 1, keepdims=False), "pipe", 1
    )
    section = section_index[None]
    first_seen = image_start[:, 0]
    run = functools.partial(layer, section=section, first_seen=first_seen)
    own = dict(rows_by_batch=own_rows, weights=own_weights)
    near = dict(rows_by_batch=near_rows, weights=near_weights)
    first = run(slot_own, states=(text_states[0],), sums=(query_sums,), **own)
    from_odd = lax.ppermute(first, "pipe", [(1, 3)])
    second = run(slot_second, states=(first,), **near)
    from_even = lax.ppermute(second, "pipe", [(0, 2)])
    ahead = run(slot_ahead, states=(from_odd,), **near)
    third = run(slot_third, states=(from_even, ahead), choosing=2, **own)
    home_odd = lax.ppermute(third, "pipe", [(3, 1)])
    fourth = run(slot_fourth, states=(third, home_odd, second), **near)
    home_even = lax.ppermute(fourth, "pipe", [(2, 0)])
    kept_state = jnp.where(section_index == 2, second, fourth)
    return jnp.where(section_index == 0, home_even, kept_state)[None]


def solution(mesh):
    sections = mesh.shape["pipe"]
    planes, far = 4, 2
    groups = mesh.shape["dp"] // (planes * far)
    mesh = Mesh(mesh.devices.reshape(planes, groups, far, sections), ("x", "z", "yh", "pipe"))
    replicas = ("x", "z", "yh")
    placed = (
        P("pipe", replicas, None),
        P(None, replicas + ("pipe",), None),
        P(None, replicas),
        P("pipe", None, None),
        P("pipe", replicas, None),
        P("pipe", replicas, None),
        P("pipe", None, None),
        P("pipe", None),
        P("pipe", None),
        P("pipe"),
    )
    return jax.shard_map(
        local, mesh=mesh, in_specs=placed, out_specs=P("pipe", replicas, None), check_vma=False
    )
```
